32 devices in a mesh: dp: 8 (over z, y), seq: 4 (over x, core).
Axes of the slice: x: 2, y: 2, z: 4, core: 2. Of those that a mesh axis runs over, the one named last changes fastest.
Arguments:
- tokens: bfloat16 [16, 2048, 768], P('dp', 'seq'), may hold values from -6 to 6
- segment_ids: int32 [16, 2048], P('dp', 'seq'), may hold values from 0 to 7, as said below
- pair_ids: int32 [16, 8], P('dp'), may hold values from 0 to 63, as said below
- w_query: bfloat16 [768, 768], replicated, may hold values from -0.21875 to 0.21875
- w_key: bfloat16 [768, 768], replicated, may hold values from -0.0390625 to 0.0390625
- w_value: bfloat16 [768, 768], replicated, may hold values from -0.21875 to 0.21875
- w_out: bfloat16 [768, 768], replicated, may hold values from -1.75 to 1.75
- w_up: bfloat16 [768, 3072], replicated, may hold values from -0.21875 to 0.21875
- w_down: bfloat16 [3072, 768], replicated, may hold values from -0.109375 to 0.109375
- w_proj: bfloat16 [768, 768], replicated, may hold values from -0.21875 to 0.21875
- gain_attn: float32 [768], replicated, may hold values from 0.5 to 1.5
- gain_ffn: float32 [768], replicated, may hold values from 0.5 to 1.5
- rel_bias: float32 [32, 12], replicated, may hold values from -4 to 4
Outputs:
- mixed: bfloat16 [16, 2048, 768], P('dp', 'seq')
- loss: float32 [], replicated
- grad_tokens: float32 [16, 2048, 768], P('dp', 'seq')
- g_query: float32 [768, 768], P('dp', 'seq')
- g_key: float32 [768, 768], P('dp', 'seq')
- g_value: float32 [768, 768], P('dp', 'seq')
- g_out: float32 [768, 768], P('dp', 'seq')
- g_up: float32 [768, 3072], P('dp', 'seq')
- g_down: float32 [3072, 768], P('dp', 'seq')
- g_proj: float32 [768, 768], P('dp', 'seq')
- g_gain_attn: float32 [768], replicated
- g_gain_ffn: float32 [768], replicated
- g_rel_bias: float32 [32, 12], replicated
The draws below stay inside these ranges and needn't reach their ends.
Inputs may be any that keep to these rules, and one draw needn't show every extreme that they name: `segment_ids`: in each row the ids never fall along the row, and every id of 0 to 7 occurs. `pair_ids`: each pair id belongs to exactly two segments among all the rows.
All inputs are finite; a program needn't handle non-finite values.
Results may differ from the reference program's by a relative error of at most 0.02.
Values may be sent and summed in bfloat16 or wider, within the bound.
A program may use at most 448 MiB of HBM per device.

```python
import jax
import jax.numpy as jnp
from jax import lax

D = 768
H = 12
DH = 64
FF = 3072
P_SIZE = 768
NB = 32
LEN = 2048
S_ROW = 8
ROWS = 16
NSEG = 128
SHORT = 73


def draw_segment_ids(key, part):
    key = jax.random.fold_in(key, 11)
    key_short, key_place = jax.random.split(key)
    short_len = jax.random.randint(key_short, (ROWS, S_ROW - 1), 1, SHORT + 1).astype(jnp.int32)
    place = jax.random.randint(key_place, (ROWS, 1), 0, S_ROW).astype(jnp.int32)
    slot = jnp.arange(S_ROW, dtype=jnp.int32)[None, :]
    filler = jnp.zeros((ROWS, 1), jnp.int32)
    before = jnp.concatenate([short_len, filler], axis=1)
    after = jnp.concatenate([filler, short_len], axis=1)
    lengths = jnp.where(slot < place, before, jnp.where(slot > place, after, 0))
    lengths = jnp.where(slot == place, LEN - jnp.sum(lengths, axis=1, keepdims=True), lengths)
    starts = jnp.cumsum(lengths, axis=1) - lengths
    position = jnp.arange(LEN, dtype=jnp.int32)[None, :, None]
    segment = jnp.sum((position >= starts[:, None, 1:]).astype(jnp.int32), axis=2)
    return segment.astype(jnp.int32)


def draw_pair_ids(key, part):
    key = jax.random.fold_in(key, 23)
    order = jax.random.permutation(key, ROWS * S_ROW)
    return (order // 2).reshape(ROWS, S_ROW).astype(jnp.int32)


def shard_levels(rng, extent, shards, low, high):
    def one(dim, parts):
        steps = jax.random.uniform(jax.random.fold_in(jax.random.fold_in(rng, 6), dim), (parts,), jnp.float32, low / len(shards), high / len(shards))
        return jnp.repeat(jnp.exp(steps), extent[dim] // parts).reshape((-1,) + (1,) * (len(extent) - dim - 1))

    factor_of = one(*shards[0])
    for cut in shards[1:]:
        factor_of = factor_of * one(*cut)
    return factor_of


def normal_values(key, extent, deviation, most, cuts=(), kind=jnp.bfloat16):
    factor_of = shard_levels(key, extent, cuts, -0.22, 0.18) if cuts else 1.0
    result = jax.random.normal(key, extent, jnp.float32) * deviation * factor_of
    return jnp.minimum(jnp.maximum(result, -most), most).astype(kind)


def setup_inputs(seed: int = 0) -> dict:
    keys = jax.random.split(jax.random.key(seed), 14)
    tokens = normal_values(keys[0], (ROWS, LEN, D), 1.0, 6.0, ((0, 8), (1, 4)))
    segment_ids = draw_segment_ids(jax.random.fold_in(keys[13], 71), 0)
    pair_ids = draw_pair_ids(jax.random.fold_in(keys[13], 71), 0)
    w_query = normal_values(keys[3], (D, D), D ** -0.5, 0.21875)
    w_key = normal_values(keys[4], (D, D), (D * 32) ** -0.5, 0.0390625)
    w_value = normal_values(keys[5], (D, D), D ** -0.5, 0.21875)
    w_out = normal_values(keys[6], (D, D), (D // 64) ** -0.5, 1.75)
    w_up = normal_values(keys[7], (D, FF), D ** -0.5, 0.21875)
    w_down = normal_values(keys[8], (FF, D), FF ** -0.5, 0.109375)
    w_proj = normal_values(keys[9], (D, P_SIZE), D ** -0.5, 0.21875)
    gain_attn = jnp.clip(1.0 + 0.1 * jax.random.normal(keys[10], (D,), jnp.float32), 0.5, 1.5)
    gain_ffn = jnp.clip(1.0 + 0.1 * jax.random.normal(keys[11], (D,), jnp.float32), 0.5, 1.5)
    rel_bias = normal_values(keys[12], (NB, H), 1.0, 4.0, (), jnp.float32)
    return {"tokens": tokens, "segment_ids": segment_ids, "pair_ids": pair_ids, "w_query": w_query, "w_key": w_key, "w_value": w_value, "w_out": w_out, "w_up": w_up, "w_down": w_down, "w_proj": w_proj, "gain_attn": gain_attn, "gain_ffn": gain_ffn, "rel_bias": rel_bias}


EPS = 1e-06
LOGIT_SCALE = 20.0
LIMITS = (12, 16, 23, 32, 46, 64, 91)
PRECISE = lax.Precision.HIGHEST

@jax.custom_vjp
def low(v):
    return lax.optimization_barrier(v.astype(jnp.bfloat16)).astype(jnp.float32)

@jax.custom_vjp
def low_back(v):
    return v

def low_keep(v):
    return (low(v), None)

def low_pass(kept, grad):
    return (grad,)

def back_keep(v):
    return (v, None)

def back_low(kept, grad):
    return (low(grad),)
low.defvjp(low_keep, low_pass)
low_back.defvjp(back_keep, back_low)

def bucket_of(offset):
    distance = jnp.abs(offset)
    beyond = 8 + sum(((distance >= bound_at).astype(jnp.int32) for bound_at in LIMITS))
    nearby = jnp.where(distance < 8, distance, beyond)
    return (nearby + NB // 2 * (offset > 0).astype(jnp.int32)).astype(jnp.int32)

def normed(inputs, gain_vec):
    return inputs * lax.rsqrt(lax.optimization_barrier(jnp.mean(inputs * inputs, axis=-1, keepdims=True)) + EPS) * gain_vec

def matmul(left, right):
    return jnp.dot(left, right, precision=PRECISE)

def reference(tokens, segment_ids, pair_ids, w_query, w_key, w_value, w_out, w_up, w_down, w_proj, gain_attn, gain_ffn, rel_bias):
    position = jnp.arange(LEN, dtype=jnp.int32)
    buckets = bucket_of(position[None, :] - position[:, None])
    member_ids = jnp.arange(S_ROW, dtype=jnp.int32)
    pair_flat = pair_ids.reshape(NSEG)
    seg_index = jnp.arange(NSEG, dtype=jnp.int32)
    self_mask = seg_index[:, None] == seg_index[None, :]
    partner = (pair_flat[:, None] == pair_flat[None, :]) & ~self_mask

    def objective(tokens_in, query_w, key_w, value_w, out_w, up_w, down_w, proj_w, gain_one, gain_two, bias_table):
        bias_full = jnp.transpose(jnp.take(bias_table, buckets, axis=0), (2, 0, 1))

        def row_step(carried, element):
            x_row, seg_row = element
            normed_one = low(normed(x_row, gain_one))
            queries = low_back(low(matmul(normed_one, query_w))).reshape(LEN, H, DH)
            key_heads = low_back(low(matmul(normed_one, key_w))).reshape(LEN, H, DH)
            value_heads = low_back(low(matmul(normed_one, value_w))).reshape(LEN, H, DH)
            scores = jnp.einsum('qhd,khd->hqk', queries, key_heads, precision=PRECISE)
            same_seg = seg_row[:, None] == seg_row[None, :]
            scores = low_back(jnp.where(same_seg[None], scores + bias_full, -1000000000.0))
            weights = low(jax.nn.softmax(scores, axis=-1))
            attended = jnp.einsum('hqk,khd->qhd', weights, value_heads, precision=PRECISE).reshape(LEN, D)
            attended = low_back(low(attended))
            hidden = x_row + low_back(matmul(attended, out_w))
            normed_two = low(normed(hidden, gain_two))
            up_proj = low_back(matmul(normed_two, up_w))
            block_out = hidden + low_back(matmul(low(jax.nn.gelu(up_proj, approximate=False)), down_w))
            member = (seg_row[None, :] == member_ids[:, None]).astype(jnp.float32)
            seg_sums = matmul(member, block_out)
            counts = lax.optimization_barrier(jnp.sum(member, axis=1))
            return (carried, (block_out, seg_sums / counts[:, None]))
        _, (block_all, pooled) = lax.scan(jax.checkpoint(row_step), jnp.float32(0.0), (tokens_in, segment_ids))
        pooled = pooled.reshape(NSEG, D)
        proj = low_back(matmul(low(pooled), proj_w))
        embed = low(proj * lax.rsqrt(lax.optimization_barrier(jnp.sum(proj * proj, axis=-1, keepdims=True)) + EPS))
        raw_scores = low_back(matmul(embed, embed.T))
        logits = LOGIT_SCALE * raw_scores
        masked = jnp.where(self_mask, -1000000000.0, logits)
        log_total = jax.nn.logsumexp(masked, axis=-1)
        positive = lax.optimization_barrier(jnp.sum(jnp.where(partner, logits, 0.0), axis=-1))
        return (jnp.mean(log_total - positive), block_all)
    float_args = (tokens.astype(jnp.float32), w_query.astype(jnp.float32), w_key.astype(jnp.float32), w_value.astype(jnp.float32), w_out.astype(jnp.float32), w_up.astype(jnp.float32), w_down.astype(jnp.float32), w_proj.astype(jnp.float32), gain_attn, gain_ffn, rel_bias)
    loss_value, pullback, block_all = jax.vjp(objective, *float_args, has_aux=True)
    gradients = pullback(jnp.ones((), jnp.float32))
    return (block_all.astype(jnp.bfloat16), loss_value, gradients[0], gradients[1], gradients[2], gradients[3], gradients[4], gradients[5], gradients[6], gradients[7], gradients[8], gradients[9], gradients[10])
```

```python
import functools

import jax
import jax.numpy as jnp
from jax import lax
from jax.experimental import pallas as pl
from jax.experimental.pallas import tpu as pltpu
from jax.sharding import PartitionSpec as P

EPS = 1e-06
LOGIT_SCALE = 20.0
LIMITS = (12, 16, 23, 32, 46, 64, 91)
MASKED = -float(2**30)
TILE = 256
SPAN = 1024
BLOCK = 128
BANDS = 5
F32 = jnp.float32
BF16 = jnp.bfloat16
MIB = 1024 * 1024


def bucket_of(offset, half_count):
    distance = jnp.abs(offset)
    beyond = 8 + sum(((distance >= bound_at).astype(jnp.int32) for bound_at in LIMITS))
    nearby = jnp.where(distance < 8, distance, beyond)
    return nearby + half_count * (offset > 0).astype(jnp.int32)


def diagonal_offsets():
    diff = (jnp.arange(BANDS, dtype=jnp.int32) - BANDS // 2)[:, None] * BLOCK
    place = jnp.arange(2 * BLOCK, dtype=jnp.int32)[None, :]
    return diff - jnp.where(place < BLOCK, place, place - 2 * BLOCK)


def dot(left, right):
    return jnp.dot(left, right, preferred_element_type=F32)


def dot_nt(left, right):
    return lax.dot_general(left, right, (((1,), (1,)), ((), ())), preferred_element_type=F32)


def three_parts(value):
    high = value.astype(BF16).astype(F32)
    rest = value - high
    middle = rest.astype(BF16).astype(F32)
    return high, middle, rest - middle


def toeplitz(vector):
    rows, size = vector, 1
    while size < BLOCK:
        rows = jnp.concatenate([rows, pltpu.roll(rows, size, 1)], axis=0)
        size *= 2
    return rows[:, :BLOCK]


def diagonal_sums(block):
    rows, size = jnp.concatenate([block, jnp.zeros_like(block)], axis=1), BLOCK
    while size > 1:
        size //= 2
        rows = rows[:size] + pltpu.roll(rows[size:], 2 * BLOCK - size, 1)
    return rows


def blocks_of(band):
    for key in range(TILE // BLOCK):
        for query in range(TILE // BLOCK):
            apart = (band - BANDS // 2) * (TILE // BLOCK) + key - query
            row = min(max(apart, -(BANDS // 2)), BANDS // 2) + BANDS // 2
            yield pl.ds(key * BLOCK, BLOCK), pl.ds(query * BLOCK, BLOCK), row


def bias_tiles(diag_ref, bias):
    rows = [diag_ref[0, row : row + 1, :] for row in range(BANDS)]
    blocks = [toeplitz(row) for row in rows[1:-1]]
    blocks = [jnp.broadcast_to(rows[0][:, :BLOCK], (BLOCK, BLOCK))] + blocks
    blocks += [jnp.broadcast_to(rows[-1][:, :BLOCK], (BLOCK, BLOCK))]
    for band in range(BANDS):
        for keys, queries, row in blocks_of(band):
            bias[band, keys, queries] = blocks[row]


def segment_rows(seg, slots, inside, outside):
    iota = lax.broadcasted_iota(jnp.int32, (slots, seg.shape[1]), 0)
    return jnp.where(iota == seg, inside, outside).astype(F32)


def extended(head, seg_part, stat_rows):
    width = head.shape[1]
    stat = jnp.concatenate(
        list(stat_rows) + [jnp.zeros((8 - len(stat_rows), width), F32)], axis=0
    )
    more = jnp.concatenate([seg_part, stat], axis=0).astype(BF16)
    rest = jnp.zeros((128 - head.shape[0] - more.shape[0], width), BF16)
    return jnp.concatenate([head, more, rest], axis=0)


def keys_side(source_ref, seg_ref, target_ref, slots):
    length = source_ref.shape[3]
    for at in range(0, length, TILE):
        part = pl.ds(at, TILE)
        seg_part = segment_rows(seg_ref[0:1, part], slots, 1.0, 0.0)
        one = jnp.ones((1, TILE), F32)
        whole = extended(source_ref[0, 0, :, part], seg_part, [one, one, one])
        whole = jnp.transpose(whole.astype(F32)).astype(BF16)
        target_ref[part, :] = whole
        target_ref[pl.ds(length + at, TILE), :] = whole


def band_of(chunk, tile):
    return jnp.clip(chunk - tile, -(BANDS // 2), BANDS // 2) + BANDS // 2


def tile_part(tile):
    return pl.ds(pl.multiple_of(tile * TILE, TILE), TILE)


def chunk_at(tile, turn, count):
    return lax.rem(tile + turn, count)


def span_part(span, tile):
    return pl.ds(pl.multiple_of(tile * TILE, TILE) + span * SPAN, SPAN)


def is_far(turn, count):
    return 2 <= turn <= count - 2


def forward_kernel(
    slots, q_ref, k_ref, v_ref, seg_ref, diag_ref, o_ref, ob_ref, inv_ref, p_ref, kx, bias, held
):
    count, spans = k_ref.shape[3] // TILE, k_ref.shape[3] // SPAN
    keys_side(k_ref, seg_ref, kx, slots)
    bias_tiles(diag_ref, bias)
    before, after = diag_ref[0, 0:1, 0:1], diag_ref[0, BANDS - 1 : BANDS, 0:1]

    def query_side(tile):
        part = tile_part(tile)
        return extended(q_ref[0, 0, :, part], segment_rows(seg_ref[0:1, part], slots, 0.0, MASKED), [])

    def score(span, tile, qx, top):
        products = dot(kx[span_part(span, tile), :], qx)
        for sub in range(SPAN // TILE):
            turn = span * (SPAN // TILE) + sub
            chunk = chunk_at(tile, turn, count)
            if is_far(turn, count):
                added = jnp.where(chunk > tile, after, before)
            else:
                added = bias[band_of(chunk, tile)]
            scores = products[sub * TILE : (sub + 1) * TILE] + added
            held[turn] = scores
            top = jnp.maximum(top, jnp.max(scores.reshape(TILE // 8, 8, TILE), axis=0))
        return top

    def weigh(turn, tile, top, total, out):
        chunk = tile_part(chunk_at(tile, turn, count))
        weights = jnp.exp(held[turn] - top)
        total = total + jnp.sum(weights.reshape(TILE // 8, 8, TILE), axis=0)
        weights = weights.astype(BF16)
        p_ref[0, chunk, tile_part(tile)] = weights
        return total, out + dot(v_ref[0, 0, :, chunk], weights)

    def finish(tile, total, out):
        part = tile_part(tile)
        inverse = 1.0 / jnp.sum(total, axis=0, keepdims=True)
        out = out * inverse
        o_ref[0, :, part] = out
        ob_ref[0, :, part] = out.astype(BF16)
        inv_ref[0, :, part] = inverse

    lowest = jnp.full((8, TILE), -jnp.inf, F32)
    start = (jnp.zeros((8, TILE), F32), jnp.zeros((v_ref.shape[2], TILE), F32))

    def body(tile, top):
        qx, following = query_side(tile + 1), lowest
        total, out = start
        for span in range(spans):
            for turn in range(span * (SPAN // TILE), (span + 1) * (SPAN // TILE)):
                total, out = weigh(turn, tile, top, total, out)
            following = score(span, tile + 1, qx, following)
        finish(tile, total, out)
        return jnp.max(following, axis=0, keepdims=True)

    qx, top = query_side(0), lowest
    for span in range(spans):
        top = score(span, 0, qx, top)
    top = lax.fori_loop(0, count - 1, body, jnp.max(top, axis=0, keepdims=True))
    total, out = start
    for turn in range(count):
        total, out = weigh(turn, count - 1, top, total, out)
    finish(count - 1, total, out)


def head_spec(rows, length):
    return pl.BlockSpec((1, rows, length), lambda h: (h, 0, 0))


def part_spec(part, width, length):
    return pl.BlockSpec((1, 1, width, length), lambda h: (h, part, 0, 0))


def attention_forward(slots, qkv, seg_row, diag):
    heads, _, width, length = qkv.shape
    return pl.pallas_call(
        functools.partial(forward_kernel, slots),
        grid=(heads,),
        in_specs=[part_spec(part, width, length) for part in range(3)]
        + [pl.BlockSpec(seg_row.shape, lambda h: (0, 0)), head_spec(8, 2 * BLOCK)],
        out_specs=[
            head_spec(width, length),
            head_spec(width, length),
            head_spec(1, length),
            head_spec(length, length),
        ],
        out_shape=[
            jax.ShapeDtypeStruct((heads, width, length), F32),
            jax.ShapeDtypeStruct((heads, width, length), BF16),
            jax.ShapeDtypeStruct((heads, 1, length), F32),
            jax.ShapeDtypeStruct((heads, length, length), BF16),
        ],
        scratch_shapes=[
            pltpu.VMEM((2 * length, 128), BF16),
            pltpu.VMEM((BANDS, TILE, TILE), F32),
            pltpu.VMEM((length // TILE, TILE, TILE), F32),
        ],
        compiler_params=pltpu.CompilerParams(
            dimension_semantics=("arbitrary",), vmem_limit_bytes=56 * MIB
        ),
        cost_estimate=pl.CostEstimate(
            flops=heads * length * length * 512,
            bytes_accessed=heads * length * (width * 12 + length * 2),
            transcendentals=heads * length * length,
        ),
        name="attention_forward",
    )(qkv, qkv, qkv, seg_row, diag)


def remote(source, target, send, receive, where):
    return pltpu.make_async_remote_copy(
        src_ref=source,
        dst_ref=target,
        send_sem=send,
        recv_sem=receive,
        device_id=where,
        device_id_type=pl.DeviceIdType.MESH,
    )


def signal(barrier, where):
    pl.semaphore_signal(barrier, inc=1, device_id=where, device_id_type=pl.DeviceIdType.MESH)


def each(first, last, step):
    def body(index, carried):
        step(index)
        return carried

    lax.fori_loop(first, last, body, 0)


def head_backward(
    q_ref,
    k_ref,
    v_ref,
    g_ref,
    o_ref,
    inv_ref,
    p_ref,
    d_ref,
    dd_ref,
    vx,
    sums,
    far,
    dkv,
    gx,
    both,
    weighed,
    left,
    beside=None,
):
    width, length = k_ref.shape[2], k_ref.shape[3]
    count, subs = length // TILE, SPAN // TILE
    for at in range(0, length, TILE):
        part = pl.ds(at, TILE)
        ones = jnp.ones((8, TILE), BF16)
        rest = jnp.zeros((128 - width - 8, TILE), BF16)
        whole = jnp.concatenate([v_ref[0, 0, :, part], ones, rest], axis=0)
        whole = jnp.transpose(whole.astype(F32)).astype(BF16)
        vx[part, :] = whole
        vx[pl.ds(length + at, TILE), :] = whole
    sums[...] = jnp.zeros_like(sums)
    far[...] = jnp.zeros_like(far)
    dkv[...] = jnp.zeros_like(dkv)
    both[1] = jnp.zeros_like(both[1])
    left[1] = jnp.zeros_like(left[1])

    def queries_side(tile, slot):
        own = tile_part(tile)
        query, grad = q_ref[0, 0, :, own], g_ref[0, :, own].astype(F32)
        inverse = inv_ref[0, :, own]
        centre = jnp.sum(grad * o_ref[0, :, own], axis=0, keepdims=True) * inverse
        grad = (grad * inverse).astype(BF16)
        stats = jnp.concatenate(list(three_parts(-centre)) + [jnp.zeros((5, TILE), F32)], axis=0)
        gx[slot] = jnp.concatenate(
            [grad, stats.astype(BF16), jnp.zeros((128 - width - 8, TILE), BF16)], axis=0
        )
        nothing = jnp.zeros((width, TILE), F32)
        upper = jnp.transpose(jnp.concatenate([query.astype(F32), nothing], axis=0))
        lower = jnp.transpose(jnp.concatenate([nothing, grad.astype(F32)], axis=0))
        both[slot] = jnp.concatenate([upper, lower], axis=0).astype(BF16)

    def weigh(tile, span, slot):
        weighed[span] = dot(vx[span_part(span, tile), :], gx[slot])

    def score(tile, span):
        for sub in range(subs):
            turn, rows = span * subs + sub, pl.ds(sub * TILE, TILE)
            chunk = chunk_at(tile, turn, count)
            weights = p_ref[0, tile_part(chunk), tile_part(tile)]
            grad_scores = weights.astype(F32) * weighed[span, rows, :]
            if is_far(turn, count):
                side = (chunk > tile).astype(jnp.int32)
                far[side] += jnp.sum(grad_scores.reshape(TILE // 8, 8, TILE), axis=0)
            else:
                sums[band_of(chunk, tile)] += grad_scores
            left[span, rows, :TILE] = grad_scores.astype(BF16)
            left[span, rows, TILE:] = weights

    def gather(tile, span, slot, grad_query):
        products = dot(left[span], both[slot])
        for sub in range(subs):
            part = tile_part(chunk_at(tile, span * subs + sub, count))
            rows = slice(sub * TILE, (sub + 1) * TILE)
            dkv[part, :] += products[rows]
            grad_query = grad_query + dot(k_ref[0, 0, :, part], left[span, rows, :TILE])
        return grad_query

    def store(tile, grad_query):
        d_ref[0, 0, :, tile_part(tile)] = grad_query.astype(BF16)

    empty = jnp.zeros((width, TILE), F32)

    def step(tile, slot, following, behind, grad_behind):
        weigh(tile, 1, slot)
        score(tile, 0)
        store(behind, gather(behind, 1, 1 - slot, grad_behind))
        queries_side(following, 1 - slot)
        weigh(following, 0, 1 - slot)
        score(tile, 1)
        return gather(tile, 0, slot, empty)

    def one(tile, carried):
        if beside is not None:
            beside(tile)
        slot = lax.rem(tile, 2)
        return step(tile, slot, lax.rem(tile + 1, count), lax.rem(tile + count - 1, count), carried)

    queries_side(0, 0)
    weigh(0, 0, 0)
    carried = lax.fori_loop(0, count, one, empty)
    store(count - 1, gather(count - 1, 1, 1, carried))
    d_both = jnp.transpose(dkv[...])
    d_ref[0, 1] = d_both[:width].astype(BF16)
    d_ref[0, 2] = d_both[width:].astype(BF16)
    totals = [None] * BANDS
    for band in range(BANDS):
        for keys, queries, row in blocks_of(band):
            block = sums[band, keys, queries]
            if row in (0, BANDS - 1):
                block = jnp.sum(block.reshape(BLOCK // 8, 8, BLOCK), axis=0)
            totals[row] = block if totals[row] is None else totals[row] + block
    for row, total in enumerate(totals):
        if row in (0, BANDS - 1):
            more = far[min(row, 1)]
            total = jnp.sum(total + more[:, :BLOCK] + more[:, BLOCK:], axis=0, keepdims=True)
            total = jnp.concatenate([total, jnp.zeros_like(total)], axis=1)
        else:
            total = diagonal_sums(total)
        dd_ref[0, row : row + 1, :] = total
    dd_ref[0, BANDS:, :] = jnp.zeros((8 - BANDS, 2 * BLOCK), F32)


def added(left, right):
    return (left.astype(F32) + right.astype(F32)).astype(BF16)


def backward_kernel(
    dp_size,
    q_ref,
    k_ref,
    v_ref,
    g_ref,
    o_ref,
    inv_ref,
    p_ref,
    normed_ref,
    up_ref,
    out_ref,
    d_ref,
    dd_ref,
    g_up_ref,
    g_out_ref,
    g_late_ref,
    last_ref,
    vx,
    sums,
    far,
    dkv,
    gx,
    both,
    weighed,
    left,
    up_near,
    out_near,
    up_far,
    out_far,
    late_out,
    late_near,
    late_total,
    late_far,
    chip_send,
    chip_recv,
    late_send,
    late_recv,
    dp_send,
    dp_recv,
):
    head, heads = pl.program_id(0), pl.num_programs(0)
    own_heads = late_near.shape[0]
    dp_at, seq_at = lax.axis_index("dp"), lax.axis_index("seq")
    chip = seq_at // 2
    rows = g_up_ref.shape[0]
    other_chip = {"dp": dp_at, "seq": lax.rem(seq_at + 2, 4)}
    peer = lambda step: {"dp": lax.rem(dp_at + step, dp_size), "seq": seq_at}
    source_of = lambda step: lax.rem(dp_at + step, dp_size)
    rows_of = lambda which: pl.ds(pl.multiple_of(which * rows, rows), rows)

    def chip_copies():
        side, there = [up_ref.at[1 - chip], out_ref.at[1 - chip]], [up_near, out_near]
        return [
            remote(source, target, chip_send.at[at], chip_recv.at[at], other_chip)
            for at, (source, target) in enumerate(zip(side, there))
        ]

    def dp_copy(kind, step, source):
        to = rows_of(lax.rem(dp_at + step, dp_size))
        if kind == 0:
            item, there = up_near.at[to, :], up_far.at[source]
        elif kind == 1:
            item, there = out_near.at[to, :], out_far.at[source]
        else:
            item, there = late_total.at[kind - 2, to, :], late_far.at[kind - 2, source]
        return remote(item, there, dp_send.at[kind, step], dp_recv.at[kind, source], peer(step))

    def late_copy(which):
        return remote(
            late_out.at[which], late_near.at[which], late_send.at[which], late_recv.at[which], other_chip
        )

    @pl.when(head == 0)
    def _():
        barrier = pltpu.get_barrier_semaphore()
        signal(barrier, other_chip)
        each(1, dp_size, lambda step: signal(barrier, peer(step)))
        pl.semaphore_wait(barrier, dp_size)
        for copy in chip_copies():
            copy.start()

    def beside(index):
        @pl.when((head == own_heads - 1) & (index == 2))
        def _():
            for copy in chip_copies():
                copy.wait_recv()

            def body(block):
                part = rows_of(block)
                up_near[part, :] = added(up_ref[chip, part, :], up_near[part, :])
                out_near[part, :] = added(out_ref[chip, part, :], out_near[part, :])

            each(0, dp_size, body)
            for kind in range(2):
                each(1, dp_size, lambda step: dp_copy(kind, step, dp_at).start())

    head_backward(
        q_ref,
        k_ref,
        v_ref,
        g_ref,
        o_ref,
        inv_ref,
        p_ref,
        d_ref,
        dd_ref,
        vx,
        sums,
        far,
        dkv,
        gx,
        both,
        weighed,
        left,
        beside,
    )
    grad_w = dot_nt(normed_ref[...], d_ref[0].reshape(-1, d_ref.shape[3]))

    @pl.when(head < own_heads)
    def _():
        late_out[head] = grad_w.astype(BF16)
        late_copy(head).start()

    for which in range(own_heads):

        @pl.when(head == own_heads + which)
        def _():
            late_copy(which).wait_recv()
            both = (grad_w + late_near[which].astype(F32)).astype(BF16)
            if which == own_heads - 1:
                last_ref[...] = both
            else:
                late_total[which] = both
                each(1, dp_size, lambda step: dp_copy(2 + which, step, dp_at).start())

    @pl.when(head == heads - 1)
    def _():
        for copy in chip_copies() + [late_copy(which) for which in range(own_heads)]:
            copy.wait_send()
        mine = rows_of(dp_at)
        totals = [
            up_near[mine, :].astype(F32),
            out_near[mine, :].astype(F32),
        ] + [late_total[which, mine, :].astype(F32) for which in range(own_heads - 1)]
        boxes = [up_far, out_far] + [late_far.at[which] for which in range(own_heads - 1)]
        for kind, box in enumerate(boxes):
            each(1, dp_size, lambda step: dp_copy(kind, step, source_of(step)).wait_recv())
            box[dp_at] = jnp.zeros(box.shape[1:], BF16)
            for source in range(dp_size):
                totals[kind] = totals[kind] + box[source].astype(F32)
            each(1, dp_size, lambda step: dp_copy(kind, step, dp_at).wait_send())
        g_up_ref[...] = totals[0]
        g_out_ref[...] = totals[1]
        for which in range(own_heads - 1):
            g_late_ref[which] = totals[2 + which]


def backward_specs(heads, width, length):
    specs = dict(
        in_specs=[part_spec(part, width, length) for part in range(3)]
        + [
            head_spec(width, length),
            head_spec(width, length),
            head_spec(1, length),
            head_spec(length, length),
        ],
        out_specs=[
            pl.BlockSpec((1, 3, width, length), lambda h: (h, 0, 0, 0)),
            head_spec(8, 2 * BLOCK),
        ],
        out_shape=[
            jax.ShapeDtypeStruct((heads, 3, width, length), BF16),
            jax.ShapeDtypeStruct((heads, 8, 2 * BLOCK), F32),
        ],
        scratch_shapes=[
            pltpu.VMEM((2 * length, 128), BF16),
            pltpu.VMEM((BANDS, TILE, TILE), F32),
            pltpu.VMEM((2, 8, TILE), F32),
            pltpu.VMEM((length, 128), F32),
            pltpu.VMEM((2, 128, TILE), BF16),
            pltpu.VMEM((2, 2 * TILE, 128), BF16),
            pltpu.VMEM((2, SPAN, TILE), F32),
            pltpu.VMEM((2, SPAN, 2 * TILE), BF16),
        ],
    )
    cost = pl.CostEstimate(
        flops=heads * length * length * 1024,
        bytes_accessed=heads * length * (width * 20 + length * 2),
        transcendentals=0,
    )
    return specs, cost


def attention_backward(qkv, g_t, o_t, inverse, probs):
    heads, _, width, length = qkv.shape
    specs, cost = backward_specs(heads, width, length)
    return pl.pallas_call(
        head_backward,
        grid=(heads,),
        compiler_params=pltpu.CompilerParams(
            dimension_semantics=("arbitrary",), vmem_limit_bytes=56 * MIB
        ),
        cost_estimate=cost,
        name="attention_backward",
        **specs,
    )(qkv, qkv, qkv, g_t, o_t, inverse, probs)


def attention_backward_and_sums(
    qkv, g_t, o_t, inverse, probs, normed_t, up_sum, out_sum, dp_size
):
    heads, _, width, length = qkv.shape
    specs, cost = backward_specs(heads, width, length)
    own_heads = heads // 2
    _, model, cols = up_sum.shape
    out_cols = out_sum.shape[2]
    rows, late = model // dp_size, 3 * width
    vmem = pl.BlockSpec(memory_space=pltpu.VMEM)
    dma = pltpu.SemaphoreType.DMA
    specs["in_specs"] += [vmem] * 3
    specs["out_specs"] += [vmem] * 4
    specs["out_shape"] += [
        jax.ShapeDtypeStruct((rows, cols), F32),
        jax.ShapeDtypeStruct((rows, out_cols), F32),
        jax.ShapeDtypeStruct((own_heads - 1, rows, late), F32),
        jax.ShapeDtypeStruct((model, late), BF16),
    ]
    specs["scratch_shapes"] += [
        pltpu.VMEM((model, cols), BF16),
        pltpu.VMEM((model, out_cols), BF16),
        pltpu.VMEM((dp_size, rows, cols), BF16),
        pltpu.VMEM((dp_size, rows, out_cols), BF16),
        pltpu.VMEM((own_heads, model, late), BF16),
        pltpu.VMEM((own_heads, model, late), BF16),
        pltpu.VMEM((own_heads - 1, model, late), BF16),
        pltpu.VMEM((own_heads - 1, dp_size, rows, late), BF16),
        dma((2,)),
        dma((2,)),
        dma((own_heads,)),
        dma((own_heads,)),
        dma((1 + own_heads, dp_size)),
        dma((1 + own_heads, dp_size)),
    ]
    return pl.pallas_call(
        functools.partial(backward_kernel, dp_size),
        grid=(heads,),
        compiler_params=pltpu.CompilerParams(
            dimension_semantics=("arbitrary",),
            vmem_limit_bytes=60 * MIB,
            collective_id=2,
            has_side_effects=True,
        ),
        cost_estimate=cost,
        name="attention_backward_and_sums",
        **specs,
    )(qkv, qkv, qkv, g_t, o_t, inverse, probs, normed_t, up_sum, out_sum)


def loss_terms(inbox, w_ref, slots, loss_ref, pooled_ref, grad_proj_ref, grad_block_ref):
    groups, _, lanes = inbox.shape
    model = 2 * (lanes - 128)
    every = inbox[...].astype(F32)
    many = groups * slots
    flat = lambda value: value.reshape(many, value.shape[2])
    pooled = jnp.concatenate(
        [flat(every[:, :slots, : model // 2]), flat(every[:, slots:, : model // 2])], axis=1
    ).astype(BF16)
    info = flat(every[:, :slots, model // 2 :])
    counts = info[:, 0:1] * 64.0 + info[:, 1:2]
    proj = dot(pooled, w_ref[...])
    inverse = lax.rsqrt(jnp.sum(proj * proj, axis=-1, keepdims=True) + EPS)
    embed = (proj * inverse).astype(BF16)
    logits = LOGIT_SCALE * dot_nt(embed, embed)
    rows_at = lax.broadcasted_iota(jnp.int32, (many, many), 0)
    self_mask = rows_at == lax.broadcasted_iota(jnp.int32, (many, many), 1)
    pairs = jnp.broadcast_to(info[:, 2:3], (many, many))
    partner = jnp.where(self_mask, 0.0, jnp.where(pairs == jnp.transpose(pairs), 1.0, 0.0))
    masked = jnp.where(self_mask, -1000000000.0, logits)
    top = jnp.max(masked, axis=-1, keepdims=True)
    log_total = top + jnp.log(jnp.sum(jnp.exp(masked - top), axis=-1, keepdims=True))
    positive = jnp.sum(jnp.where(partner > 0.0, logits, 0.0), axis=-1, keepdims=True)
    loss = jnp.sum(log_total - positive, axis=0, keepdims=True) / many
    loss_ref[...] = jnp.broadcast_to(loss, loss_ref.shape)
    grad_raw = LOGIT_SCALE * ((jnp.exp(masked - log_total) - partner) / many)
    grad_raw = grad_raw.astype(BF16)
    turned = jnp.transpose(grad_raw.astype(F32)).astype(BF16)
    grad_embed = dot(grad_raw, embed) + dot(turned, embed)
    inner = jnp.sum(proj * grad_embed, axis=-1, keepdims=True)
    grad_proj = inverse * grad_embed - inverse * inverse * inverse * proj * inner
    grad_proj = grad_proj.astype(BF16)
    pooled_ref[...] = pooled
    grad_proj_ref[...] = grad_proj
    grad_block_ref[...] = dot_nt(grad_proj, w_ref[...]) / counts


def head_kernel(
    dp_size,
    seq_size,
    sums_ref,
    act_ref,
    info_ref,
    w_ref,
    loss_ref,
    pooled_ref,
    grad_proj_ref,
    grad_block_ref,
    act_all_ref,
    near_sums,
    near_act,
    act_total,
    inbox,
    act_inbox,
    near_send,
    near_recv,
    far_send,
    far_recv,
):
    half, groups = seq_size // 2, 2 * dp_size
    dp_at, seq_at = lax.axis_index("dp"), lax.axis_index("seq")
    row, turn = seq_at // half, lax.rem(seq_at, half)
    me = dp_at * 2 + row
    model = sums_ref.shape[1]
    slots = sums_ref.shape[0]

    def member(step):
        return lax.rem(turn + step, half)

    def sibling(step):
        return {"dp": dp_at, "seq": row * half + member(step)}

    def group(step):
        return lax.rem(me + step, groups)

    def peer(step):
        other = group(step)
        return {"dp": other // 2, "seq": lax.rem(other, 2) * half + turn}

    barrier = pltpu.get_barrier_semaphore()
    for step in range(1, half):
        signal(barrier, sibling(step))
    each(1, groups, lambda step: signal(barrier, peer(step)))
    near_sums[turn] = sums_ref[...]
    near_act[turn] = act_ref[...]
    pl.semaphore_wait(barrier, half - 1 + groups - 1)

    def near(step, source):
        return [
            remote(
                buffer.at[source],
                buffer.at[source],
                near_send.at[kind, step],
                near_recv.at[kind, source],
                sibling(step),
            )
            for kind, buffer in enumerate((near_sums, near_act))
        ]

    for step in range(1, half):
        for copy in near(step, turn):
            copy.start()
    for step in range(1, half):
        for copy in near(step, member(step)):
            copy.wait_recv()
    sums, act = near_sums[0], near_act[0]
    for source in range(1, half):
        sums, act = sums + near_sums[source], act + near_act[source]
    info = info_ref[...]
    pooled = sums / (info[:, 0:1] * 64.0 + info[:, 1:2])
    inbox[me] = jnp.concatenate(
        [
            jnp.concatenate([pooled[:, : model // 2], info], axis=1),
            jnp.concatenate([pooled[:, model // 2 :], jnp.zeros_like(info)], axis=1),
        ],
        axis=0,
    ).astype(BF16)
    act_total[...] = act
    act_inbox[me] = act_total[dp_at]

    def message(step, source):
        return remote(
            inbox.at[source], inbox.at[source], far_send.at[0, step], far_recv.at[0, source], peer(step)
        )

    def act_message(step, source):
        return remote(
            act_total.at[group(step) // 2],
            act_inbox.at[source],
            far_send.at[1, step],
            far_recv.at[1, source],
            peer(step),
        )

    each(1, groups, lambda step: message(step, me).start())
    each(1, groups, lambda step: act_message(step, me).start())
    each(1, groups, lambda step: message(step, group(step)).wait_recv())

    loss_terms(inbox, w_ref, slots, loss_ref, pooled_ref, grad_proj_ref, grad_block_ref)
    each(1, groups, lambda step: act_message(step, group(step)).wait_recv())
    act_all_ref[...] = act_inbox[...]
    for step in range(1, half):
        for copy in near(step, turn):
            copy.wait_send()
    each(1, groups, lambda step: message(step, me).wait_send())
    each(1, groups, lambda step: act_message(step, me).wait_send())


def loss_head(sums, act_sums, info, w_proj, dp_size, seq_size):
    slots, model = sums.shape
    groups, half, many = 2 * dp_size, seq_size // 2, 2 * dp_size * slots
    cols = act_sums.shape[1] // dp_size
    act_parts = act_sums.reshape(slots, dp_size, cols).transpose(1, 0, 2)
    vmem = pl.BlockSpec(memory_space=pltpu.VMEM)
    return pl.pallas_call(
        functools.partial(head_kernel, dp_size, seq_size),
        in_specs=[vmem] * 4,
        out_specs=[vmem] * 5,
        out_shape=[
            jax.ShapeDtypeStruct((8, 128), F32),
            jax.ShapeDtypeStruct((many, model), BF16),
            jax.ShapeDtypeStruct((many, w_proj.shape[1]), BF16),
            jax.ShapeDtypeStruct((many, model), F32),
            jax.ShapeDtypeStruct((groups, slots, cols), F32),
        ],
        scratch_shapes=[
            pltpu.VMEM((half, slots, model), F32),
            pltpu.VMEM((half, dp_size, slots, cols), F32),
            pltpu.VMEM((dp_size, slots, cols), F32),
            pltpu.VMEM((groups, 2 * slots, model // 2 + 128), BF16),
            pltpu.VMEM((groups, slots, cols), F32),
            pltpu.SemaphoreType.DMA((2, half)),
            pltpu.SemaphoreType.DMA((2, half)),
            pltpu.SemaphoreType.DMA((2, groups)),
            pltpu.SemaphoreType.DMA((2, groups)),
        ],
        compiler_params=pltpu.CompilerParams(
            collective_id=0, has_side_effects=True, vmem_limit_bytes=40 * MIB
        ),
        cost_estimate=pl.CostEstimate(
            flops=4 * many * model * model, bytes_accessed=8 * MIB, transcendentals=many * many
        ),
        name="loss_head",
    )(sums, act_parts, info, w_proj)


def total_kernel(
    dp_size, seq_size, value_ref, out_ref, seq_box, dp_box, seq_send, seq_recv, dp_send, dp_recv
):
    dp_at, seq_at = lax.axis_index("dp"), lax.axis_index("seq")
    along_seq = lambda step: {"dp": dp_at, "seq": lax.rem(seq_at + step, seq_size)}
    along_dp = lambda step: {"dp": lax.rem(dp_at + step, dp_size), "seq": seq_at}
    barrier = pltpu.get_barrier_semaphore()
    each(1, seq_size, lambda step: signal(barrier, along_seq(step)))
    each(1, dp_size, lambda step: signal(barrier, along_dp(step)))
    pl.semaphore_wait(barrier, seq_size - 1 + dp_size - 1)

    def stage(value, at, size, where, box, send, receive):
        box[at] = value
        copy = lambda step, source: remote(
            box.at[source], box.at[source], send.at[step], receive.at[source], where(step)
        )
        each(1, size, lambda step: copy(step, at).start())
        each(1, size, lambda step: copy(step, lax.rem(at + step, size)).wait_recv())
        total = box[0]
        for source in range(1, size):
            total = total + box[source]
        each(1, size, lambda step: copy(step, at).wait_send())
        return total

    value = stage(value_ref[...], seq_at, seq_size, along_seq, seq_box, seq_send, seq_recv)
    out_ref[...] = stage(value, dp_at, dp_size, along_dp, dp_box, dp_send, dp_recv)


def total_over_all(value, dp_size, seq_size):
    vmem = pl.BlockSpec(memory_space=pltpu.VMEM)
    return pl.pallas_call(
        functools.partial(total_kernel, dp_size, seq_size),
        in_specs=[vmem],
        out_specs=vmem,
        out_shape=jax.ShapeDtypeStruct(value.shape, F32),
        scratch_shapes=[
            pltpu.VMEM((seq_size,) + value.shape, F32),
            pltpu.VMEM((dp_size,) + value.shape, F32),
            pltpu.SemaphoreType.DMA((seq_size,)),
            pltpu.SemaphoreType.DMA((seq_size,)),
            pltpu.SemaphoreType.DMA((dp_size,)),
            pltpu.SemaphoreType.DMA((dp_size,)),
        ],
        compiler_params=pltpu.CompilerParams(collective_id=1, has_side_effects=True),
        name="total_over_all",
    )(value)


def front_kernel(
    tokens_ref,
    seg_ref,
    pair_ref,
    gain_ref,
    wq_hbm,
    wk_hbm,
    wv_hbm,
    qkv_hbm,
    normed_hbm,
    own_hbm,
    row_ref,
    w_own_hbm,
    info_ref,
    column_ref,
    qkv_ref,
    normed_ref,
    w_own_ref,
    x_all,
    seg_here,
    seg_all,
    weights,
    turned,
    w_t,
    load_sem,
    store_sem,
    x_send,
    x_recv,
    seg_send,
    seg_recv,
):
    seq_at = lax.axis_index("seq")
    dp_at = lax.axis_index("dp")
    row, turn = seq_at // 2, lax.rem(seq_at, 2)
    other_core = {"dp": dp_at, "seq": row * 2 + 1 - turn}
    other_chip = {"dp": dp_at, "seq": lax.rem(seq_at + 2, 4)}
    piece, model = x_all.shape[1:]
    width = 64
    halves = piece // TILE
    heads = w_t.shape[0] // (3 * width)
    block_cols = heads // 2 * width
    loads = [
        pltpu.make_async_copy(source, weights.at[at], load_sem.at[at])
        for at, source in enumerate((wq_hbm, wk_hbm, wv_hbm))
    ]
    barrier = pltpu.get_barrier_semaphore()
    signal(barrier, other_core)
    signal(barrier, other_chip)
    for load in loads:
        load.start()
    for at in range(2):
        seg_here[at] = jnp.broadcast_to(seg_ref[at : at + 1, :], seg_here.shape[1:])
    pl.semaphore_wait(barrier, 2)

    def part_of(half):
        return tile_part(half)

    def chip_copy(half, slot):
        return remote(
            tokens_ref.at[1 - row, part_of(half), :],
            x_all.at[slot, part_of(half), :],
            x_send.at[0, half],
            x_recv.at[0, half],
            other_chip,
        )

    def core_copy(kind, half, slot):
        source = tokens_ref.at[row, part_of(half), :] if kind == 1 else x_all.at[slot, part_of(half), :]
        return remote(
            source,
            x_all.at[slot, part_of(half), :],
            x_send.at[kind, half],
            x_recv.at[kind, half],
            other_core,
        )

    def seg_copy(kind, slot):
        source = [seg_here.at[1 - row], seg_here.at[row], seg_all.at[slot]][kind]
        where = other_chip if kind == 0 else other_core
        return remote(source, seg_all.at[slot], seg_send.at[kind], seg_recv.at[kind], where)

    mine, partner = seq_at, lax.rem(seq_at + 2, 4)
    beside, beyond = row * 2 + 1 - turn, lax.rem(row * 2 + 1 - turn + 2, 4)
    for half in range(halves):
        chip_copy(half, mine).start()
    for half in range(halves):
        core_copy(1, half, mine).start()
    seg_copy(0, mine).start()
    seg_copy(1, mine).start()
    x_all[mine] = tokens_ref[row]
    seg_all[mine] = seg_here[row]

    for load in loads:
        load.wait()
    for at in range(3):

        def turn_strip(strip):
            part = tile_part(strip)
            turned[part, :] = jnp.transpose(weights[at, :, part].astype(F32)).astype(BF16)

        each(0, model // TILE, turn_strip)
        for head in range(heads):
            block = head // (heads // 2)
            which = 1 - row if block == 0 else row
            start = pl.multiple_of((which * 2 + turn) * block_cols, block_cols)
            start = start + head % (heads // 2) * width
            w_t[pl.ds((head * 3 + at) * width, width), :] = turned[pl.ds(start, width), :]
    gain = gain_ref[...].reshape(1, model)

    def project(slot, half):
        part = tile_part(half)
        x = x_all[slot, part, :].astype(F32)
        scale = lax.rsqrt(jnp.mean(x * x, axis=1, keepdims=True) + EPS)
        normed_part = jnp.transpose(x * scale * gain).astype(BF16)
        lanes = pl.ds(pl.multiple_of(slot * piece + half * TILE, TILE), TILE)
        normed_ref[:, lanes] = normed_part
        qkv_ref[:, lanes] = dot(w_t[...], normed_part).astype(BF16)

    def results(slot, at):
        lanes = pl.ds(pl.multiple_of(slot * piece, piece), piece)
        return [
            pltpu.make_async_copy(source.at[:, lanes], target.at[:, lanes], store_sem.at[kind, at])
            for kind, (source, target) in enumerate([(qkv_ref, qkv_hbm), (normed_ref, normed_hbm)])
        ]

    order = (mine, beside, partner, beyond)
    own_copies = [
        pltpu.make_async_copy(
            x_all.at[turn + 2 * which], own_hbm.at[pl.ds(which * piece, piece), :], store_sem.at[2, which]
        )
        for which in range(2)
    ] + [pltpu.make_async_copy(w_own_ref, w_own_hbm, store_sem.at[2, 2])]

    def unit(at):
        which, half = at // halves, lax.rem(at, halves)
        slot = jnp.where(which == 0, mine, jnp.where(which == 1, beside, jnp.where(which == 2, partner, beyond)))

        @pl.when(which == 1)
        def _():
            core_copy(1, half, beside).wait_recv()

        @pl.when(at == 2 * halves)
        def _():
            def turn_back(strip):
                part = pl.ds(pl.multiple_of(strip * BLOCK, BLOCK), BLOCK)
                w_own_ref[:, part] = jnp.transpose(w_t[part, :].astype(F32)).astype(BF16)

            each(0, w_t.shape[0] // BLOCK, turn_back)
            own_copies[2].start()
            seg_copy(0, partner).wait_recv()
            seg_copy(2, partner).start()

        @pl.when(which == 2)
        def _():
            chip_copy(half, partner).wait_recv()
            core_copy(2, half, partner).start()

        @pl.when(which == 3)
        def _():
            core_copy(2, half, beyond).wait_recv()

        project(slot, half)

        @pl.when(half == halves - 1)
        def _():
            for copy in results(slot, which):
                copy.start()

    each(0, 4 * halves, unit)
    for copy in own_copies[:2]:
        copy.start()
    seg_copy(1, beside).wait_recv()
    seg_copy(2, beyond).wait_recv()
    slots = info_ref.shape[0]
    ids = lax.broadcasted_iota(jnp.int32, (slots, piece), 0)
    counts = jnp.zeros((slots, 1), F32)
    for slot in range(4):
        row_ref[:, pl.ds(slot * piece, piece)] = seg_all[slot]
        hit = jnp.where(seg_all[slot] == ids, 1.0, 0.0)
        counts = counts + jnp.sum(hit, axis=1, keepdims=True)
    for which in range(2):
        column = jnp.transpose(jnp.broadcast_to(seg_all[turn + 2 * which, 0:1, :].astype(F32), (128, piece)))
        column_ref[pl.ds(which * piece, piece), :] = column.astype(jnp.int32)
    lane = lax.broadcasted_iota(jnp.int32, info_ref.shape, 1)
    own_pairs = jnp.broadcast_to(pair_ref[pl.ds(row, 1), :].astype(F32), (slots, slots))
    square = lax.broadcasted_iota(jnp.int32, (slots, slots), 0)
    square = square == lax.broadcasted_iota(jnp.int32, (slots, slots), 1)
    own_pairs = jnp.sum(jnp.where(square, own_pairs, 0.0), axis=1, keepdims=True)
    high = jnp.floor(counts * (1.0 / 64.0))
    info = jnp.where(lane == 0, high, jnp.where(lane == 1, counts - 64.0 * high, 0.0))
    info_ref[...] = jnp.where(lane == 2, own_pairs, info)
    for half in range(halves):
        chip_copy(half, mine).wait_send()
        core_copy(1, half, mine).wait_send()
        core_copy(2, half, partner).wait_send()
    for kind, slot in enumerate((mine, mine, partner)):
        seg_copy(kind, slot).wait_send()
    for copy in own_copies + [copy for at, slot in enumerate(order) for copy in results(slot, at)]:
        copy.wait()


def gather_and_project(tokens, segment_ids, pair_ids, gain, w_query, w_key, w_value, heads):
    _, piece, model = tokens.shape
    columns, length = 3 * heads * 64, 4 * piece
    vmem, anywhere = pl.BlockSpec(memory_space=pltpu.VMEM), pl.BlockSpec(memory_space=pl.ANY)
    dma = pltpu.SemaphoreType.DMA
    return pl.pallas_call(
        front_kernel,
        in_specs=[vmem] * 4 + [anywhere] * 3,
        out_specs=[anywhere] * 3 + [vmem, anywhere, vmem, vmem],
        out_shape=[
            jax.ShapeDtypeStruct((columns, length), BF16),
            jax.ShapeDtypeStruct((model, length), BF16),
            jax.ShapeDtypeStruct((2 * piece, model), BF16),
            jax.ShapeDtypeStruct((8, length), jnp.int32),
            jax.ShapeDtypeStruct((model, columns), BF16),
            jax.ShapeDtypeStruct((pair_ids.shape[1], 128), F32),
            jax.ShapeDtypeStruct((2 * piece, 128), jnp.int32),
        ],
        scratch_shapes=[
            pltpu.VMEM((columns, length), BF16),
            pltpu.VMEM((model, length), BF16),
            pltpu.VMEM((model, columns), BF16),
            pltpu.VMEM((4, piece, model), BF16),
            pltpu.VMEM((2, 8, piece), jnp.int32),
            pltpu.VMEM((4, 8, piece), jnp.int32),
            pltpu.VMEM((3, model, model), BF16),
            pltpu.VMEM((model, model), BF16),
            pltpu.VMEM((columns, model), BF16),
            dma((3,)),
            dma((3, 4)),
            dma((3, piece // TILE)),
            dma((3, piece // TILE)),
            dma((3,)),
            dma((3,)),
        ],
        compiler_params=pltpu.CompilerParams(
            collective_id=5, has_side_effects=True, vmem_limit_bytes=63 * MIB
        ),
        cost_estimate=pl.CostEstimate(
            flops=2 * columns * length * model, bytes_accessed=20 * MIB, transcendentals=0
        ),
        name="gather_and_project",
    )(
        tokens,
        segment_ids,
        pair_ids,
        gain,
        w_query,
        w_key,
        w_value,
    )


def middle_kernel(
    dp_size,
    info_ref,
    seg_ref,
    gain_ref,
    w_out_hbm,
    x_hbm,
    w_up_hbm,
    w_down_hbm,
    w_proj_hbm,
    o_hbm,
    mixed_ref,
    loss_ref,
    pooled_ref,
    grad_proj_ref,
    grad_block_ref,
    act_all_ref,
    g_ref,
    grad_hbm,
    gain_sum,
    up_ref,
    out_ref,
    w_out,
    x_own,
    w_up,
    w_down,
    w_proj,
    attended,
    hidden,
    normed_two,
    normed_t,
    act,
    slope,
    total,
    members_t,
    sum_parts,
    mixed_out,
    near_sums,
    near_act,
    act_total,
    inbox,
    act_inbox,
    grad_b,
    grad_att,
    out_send,
    out_recv,
    load_sem,
    store_sem,
    head_load,
    head_send,
    head_recv,
    near_send,
    near_recv,
    far_send,
    far_recv,
    mixed_send,
    mixed_recv,
    att_send,
    att_recv,
    core_send,
    core_recv,
):
    dp_at, seq_at = lax.axis_index("dp"), lax.axis_index("seq")
    row, turn = seq_at // 2, lax.rem(seq_at, 2)
    groups, me = 2 * dp_size, dp_at * 2 + row
    other_core = {"dp": dp_at, "seq": row * 2 + 1 - turn}
    other_chip = {"dp": dp_at, "seq": lax.rem(seq_at + 2, 4)}
    group = lambda step: lax.rem(me + step, groups)
    peer = lambda step: {"dp": group(step) // 2, "seq": lax.rem(group(step), 2) * 2 + turn}
    tokens, model = hidden.shape
    slots = info_ref.shape[0]
    piece, units = tokens // 2, w_up.shape[1]
    cols, out_cols = up_ref.shape[2], out_ref.shape[2]
    act_cols = units // dp_size
    pairs = [
        (w_out_hbm, w_out),
        (x_hbm, x_own),
        (w_up_hbm, w_up),
        (w_down_hbm, w_down),
        (w_proj_hbm, w_proj),
    ]
    loads = [pltpu.make_async_copy(*pair, load_sem.at[at]) for at, pair in enumerate(pairs)]
    barrier = pltpu.get_barrier_semaphore()
    signal(barrier, other_core)
    each(1, groups, lambda step: signal(barrier, peer(step)))

    def head_rows(member, block):
        which = 1 - row if block == 0 else row
        return pl.ds(pl.multiple_of((which * 2 + member) * out_cols, out_cols), out_cols)

    def row_lanes(member, half):
        return pl.ds(pl.multiple_of((member + 2 * half) * piece, piece), piece)

    def half_of(half):
        return pl.ds(pl.multiple_of(half * piece, piece), piece)

    def heads_here(block, half):
        return pltpu.make_async_copy(
            o_hbm.at[pl.ds(block * out_cols, out_cols), row_lanes(turn, half)],
            attended.at[head_rows(turn, block), half_of(half)],
            head_load.at[block, half],
        )

    def heads_there(block, half, sender):
        return remote(
            o_hbm.at[pl.ds(block * out_cols, out_cols), row_lanes(1 - sender, half)],
            attended.at[head_rows(sender, block), half_of(half)],
            head_send.at[block, half],
            head_recv.at[block, half],
            other_core,
        )

    quarters = [(block, half) for half in range(2) for block in range(2)]
    for block, half in quarters:
        heads_here(block, half).start()
    for load in loads:
        load.start()
    pl.semaphore_wait(barrier, groups)
    for block, half in quarters:
        heads_there(block, half, turn).start()

    def members(rows, parts):
        seg = seg_ref[rows, :]
        lane = lax.broadcasted_iota(jnp.int32, seg.shape, 1)
        hit = (lax.rem(lane, 16) == seg) & (lane < 16 * parts)
        return jnp.where(hit, 1.0, 0.0)

    gain = gain_ref[...].reshape(1, model)
    loads[0].wait()
    loads[1].wait()
    per_half = piece // TILE

    def attended_tile(at):
        @pl.when(lax.rem(at, per_half) == 0)
        def _():
            for block in range(2):
                heads_here(block, at // per_half).wait()
                heads_there(block, at // per_half, 1 - turn).wait_recv()

        rows = tile_part(at)
        left = jnp.transpose(attended[:, rows].astype(F32)).astype(BF16)
        value = x_own[rows, :].astype(F32) + dot(left, w_out[...])
        hidden[rows, :] = value
        scale = lax.rsqrt(jnp.mean(value * value, axis=1, keepdims=True) + EPS)
        value = value * scale * gain
        normed_two[rows, :] = value.astype(BF16)
        normed_t[:, rows] = jnp.transpose(value).astype(BF16)

    each(0, tokens // TILE, attended_tile)
    loads[2].wait()

    def up(at):
        lanes = tile_part(at)
        for half in range(2):
            rows = half_of(half)
            value = dot(normed_two[rows, :], w_up[:, lanes])
            below = 0.5 + 0.5 * lax.erf(value * (0.5**0.5))
            density = jnp.exp(-0.5 * value * value) * 0.3989422804014327
            act[rows, lanes] = (value * below).astype(BF16)
            slope[rows, lanes] = (below + value * density).astype(BF16)

    each(0, units // TILE, up)
    loads[3].wait()
    member = jnp.transpose(members(pl.ds(0, tokens), 1))[:16].astype(BF16)
    sum_parts[...] = jnp.zeros_like(sum_parts)

    def down(half):
        rows = pl.ds(pl.multiple_of(half * piece, piece), piece)
        value = hidden[rows, :] + dot(act[rows, :], w_down[...])
        total[rows, :] = value
        high = value.astype(BF16)
        rest = (value - high.astype(F32)).astype(BF16)
        left = members_t[:, rows]
        sum_parts[...] += dot(left, high) + dot(left, rest)

    members_t[...] = member
    each(0, 2, down)
    near_sums[turn] = sum_parts[:slots, :]

    def act_part(part):
        lanes = pl.ds(pl.multiple_of(part * act_cols, act_cols), act_cols)
        near_act[turn, part] = dot(members_t[...], act[:, lanes])[:slots]

    each(0, dp_size, act_part)

    def near(source):
        return [
            remote(
                buffer.at[source],
                buffer.at[source],
                near_send.at[kind],
                near_recv.at[kind],
                other_core,
            )
            for kind, buffer in enumerate((near_sums, near_act))
        ]

    for copy in near(turn):
        copy.start()
    mixed_ref[row] = total[pl.ds(pl.multiple_of(row * piece, piece), piece), :].astype(BF16)
    mixed_out[...] = total[pl.ds(pl.multiple_of((1 - row) * piece, piece), piece), :].astype(BF16)
    mixed_copy = lambda at: remote(
        mixed_out, mixed_ref.at[at], mixed_send.at[0], mixed_recv.at[0], other_chip
    )
    for copy in near(1 - turn):
        copy.wait_recv()
    info = info_ref[...]
    pooled = (near_sums[0] + near_sums[1]) / (info[:, 0:1] * 64.0 + info[:, 1:2])
    inbox[me] = jnp.concatenate(
        [
            jnp.concatenate([pooled[:, : model // 2], info], axis=1),
            jnp.concatenate([pooled[:, model // 2 :], jnp.zeros_like(info)], axis=1),
        ],
        axis=0,
    ).astype(BF16)

    def message(step, source):
        return remote(
            inbox.at[source], inbox.at[source], far_send.at[0, step], far_recv.at[0, source], peer(step)
        )

    def act_message(step, source):
        return remote(
            act_total.at[group(step) // 2],
            act_inbox.at[source],
            far_send.at[1, step],
            far_recv.at[1, source],
            peer(step),
        )

    each(1, groups, lambda step: message(step, me).start())
    act_total[...] = near_act[0] + near_act[1]
    act_inbox[me] = act_total[dp_at]
    loads[4].wait()
    each(1, groups, lambda step: message(step, group(step)).wait_recv())
    each(1, groups, lambda step: act_message(step, me).start())
    mixed_copy(row).start()
    loss_terms(inbox, w_proj, slots, loss_ref, pooled_ref, grad_proj_ref, grad_block_ref)

    def stacked(parts):
        parts = [part.astype(BF16) for part in parts]
        rest = jnp.zeros((128 - 16 * len(parts), parts[0].shape[1]), BF16)
        return jnp.concatenate(parts + [rest], axis=0)

    block = grad_block_ref[pl.ds(pl.multiple_of(me * slots, slots), slots), :]
    block = jnp.concatenate([block, jnp.zeros_like(block)], axis=0)
    block_b, block_parts = block.astype(BF16), stacked(three_parts(block))

    def grad_up(at):
        lanes = tile_part(at)
        grad_act = dot_nt(block_b, w_down[lanes, :])
        high = grad_act.astype(BF16).astype(F32)
        both = stacked([high, grad_act - high])
        for half in range(2):
            rows = half_of(half)
            spread = dot(members(rows, 2).astype(BF16), both)
            slope[rows, lanes] = (spread * slope[rows, lanes].astype(F32)).astype(BF16)

    each(0, units // TILE, grad_up)
    gain_sum[...] = jnp.zeros_like(gain_sum)

    def token_part(at):
        rows = pl.ds(pl.multiple_of(at * BLOCK, BLOCK), BLOCK)
        grad, value = total[rows, :], hidden[rows, :]
        scale = lax.rsqrt(jnp.mean(value * value, axis=1, keepdims=True) + EPS)
        scaled = gain * grad
        inner = jnp.mean(scaled * value, axis=1, keepdims=True)
        terms = grad * value * scale
        gain_sum[...] += jnp.sum(terms.reshape(BLOCK // 8, 8, model), axis=0)
        result = dot(members(rows, 3).astype(BF16), block_parts)
        result = result + scale * scaled - value * (scale * scale * scale * inner)
        total[rows, :] = result
        grad_b[rows, :] = result.astype(BF16)

    def att_copy(block, half, sender):
        return remote(
            grad_att.at[head_rows(1 - sender, block), half_of(half)],
            g_ref.at[pl.ds(block * out_cols, out_cols), row_lanes(sender, half)],
            att_send.at[block, half],
            att_recv.at[block, half],
            other_core,
        )

    def store(half):
        return pltpu.make_async_copy(
            total.at[half_of(half), :], grad_hbm.at[half_of(half), :], store_sem.at[half]
        )

    def token_half(half):
        rows = half_of(half)
        total[rows, :] = dot_nt(slope[rows, :], w_up[...])
        each(half * (piece // BLOCK), (half + 1) * (piece // BLOCK), token_part)
        store(half).start()
        grad_att[:, rows] = dot_nt(w_out[...], grad_b[rows, :]).astype(BF16)
        for block in range(2):
            att_copy(block, half, turn).start()

    each(0, 2, token_half)
    for block, half in quarters:
        mine = grad_att[head_rows(turn, block), half_of(half)]
        g_ref[pl.ds(block * out_cols, out_cols), row_lanes(turn, half)] = mine

    def up_box(kind, x):
        return act.at[pl.ds(0, model), pl.ds(pl.multiple_of((2 * kind + x) * cols, cols), cols)]

    def up_copy(x):
        return remote(up_box(0, x), up_box(1, x), core_send.at[0, x], core_recv.at[0, x], other_core)

    def out_copy(x):
        return remote(
            out_send.at[x], out_recv.at[x], core_send.at[1, x], core_recv.at[1, x], other_core
        )

    def out_part(x, core):
        starts = [(2 * x + side) * out_cols for side in range(2)]
        return jnp.where(core == 0, *(out_full[:, start : start + out_cols] for start in starts))

    strips = cols // TILE

    def up_strip(at):
        side, x = at // (2 * strips), lax.rem(at // strips, 2)
        strip = lax.rem(at, strips)
        core = jnp.where(side == 0, 1 - turn, turn)
        start = pl.multiple_of((2 * x + core) * cols + strip * TILE, TILE)
        value = dot(normed_t[...], slope[:, pl.ds(start, TILE)]).astype(BF16)

        @pl.when(side == 0)
        def _():
            act[:model, pl.ds(pl.multiple_of(x * cols + strip * TILE, TILE), TILE)] = value

            @pl.when(strip == strips - 1)
            def _():
                up_copy(x).start()

        @pl.when(side == 1)
        def _():
            up_ref[x, :, tile_part(strip)] = value

    each(0, 2 * strips, up_strip)
    out_full = dot(attended[...], grad_b[...])
    for x in range(2):
        out_send[x] = out_part(x, 1 - turn).astype(BF16)
        out_copy(x).start()
    each(2 * strips, 4 * strips, up_strip)
    for x in range(2):
        up_copy(x).wait_recv()
        out_copy(x).wait_recv()
        up_ref[x] = added(up_ref[x], act[:model, (2 + x) * cols : (3 + x) * cols])
        out_ref[x] = (out_part(x, turn) + out_recv[x].astype(F32)).astype(BF16)

    mixed_copy(1 - row).wait_recv()
    each(1, groups, lambda step: act_message(step, group(step)).wait_recv())
    act_all_ref[...] = act_inbox[...]
    for block, half in quarters:
        att_copy(block, half, 1 - turn).wait_recv()
        att_copy(block, half, turn).wait_send()
        heads_there(block, half, turn).wait_send()
    for x in range(2):
        up_copy(x).wait_send()
        out_copy(x).wait_send()
    for copy in near(turn):
        copy.wait_send()
    mixed_copy(row).wait_send()
    each(1, groups, lambda step: message(step, me).wait_send())
    each(1, groups, lambda step: act_message(step, me).wait_send())
    for half in range(2):
        store(half).wait()


def feed_forward_and_loss(info, seg_columns, gain, w_out, x_own, w_up, w_down, w_proj, o_t, dp_size):
    slots = info.shape[0]
    tokens, model = x_own.shape
    units, piece = w_up.shape[1], tokens // 2
    cols, out_cols = units // 4, model // 4
    groups, many, act_cols = 2 * dp_size, 2 * dp_size * slots, units // dp_size
    vmem, anywhere = pl.BlockSpec(memory_space=pltpu.VMEM), pl.BlockSpec(memory_space=pl.ANY)
    dma, shape = pltpu.SemaphoreType.DMA, jax.ShapeDtypeStruct
    return pl.pallas_call(
        functools.partial(middle_kernel, dp_size),
        in_specs=[vmem] * 3 + [anywhere] * 6,
        out_specs=[vmem] * 7 + [anywhere] + [vmem] * 3,
        out_shape=[
            shape((2, piece, model), BF16),
            shape((8, 128), F32),
            shape((many, model), BF16),
            shape((many, w_proj.shape[1]), BF16),
            shape((many, model), F32),
            shape((groups, slots, act_cols), F32),
            shape((2 * out_cols, 2 * tokens), BF16),
            shape((tokens, model), F32),
            shape((8, model), F32),
            shape((2, model, cols), BF16),
            shape((2, model, out_cols), BF16),
        ],
        scratch_shapes=[
            pltpu.VMEM((model, model), BF16),
            pltpu.VMEM((tokens, model), BF16),
            pltpu.VMEM((model, units), BF16),
            pltpu.VMEM((units, model), BF16),
            pltpu.VMEM(w_proj.shape, BF16),
            pltpu.VMEM((model, tokens), BF16),
            pltpu.VMEM((tokens, model), F32),
            pltpu.VMEM((tokens, model), BF16),
            pltpu.VMEM((model, tokens), BF16),
            pltpu.VMEM((tokens, units), BF16),
            pltpu.VMEM((tokens, units), BF16),
            pltpu.VMEM((tokens, model), F32),
            pltpu.VMEM((16, tokens), BF16),
            pltpu.VMEM((16, model), F32),
            pltpu.VMEM((piece, model), BF16),
            pltpu.VMEM((2, slots, model), F32),
            pltpu.VMEM((2, dp_size, slots, act_cols), F32),
            pltpu.VMEM((dp_size, slots, act_cols), F32),
            pltpu.VMEM((groups, 2 * slots, model // 2 + 128), BF16),
            pltpu.VMEM((groups, slots, act_cols), F32),
            pltpu.VMEM((tokens, model), BF16),
            pltpu.VMEM((model, tokens), BF16),
            pltpu.VMEM((2, model, out_cols), BF16),
            pltpu.VMEM((2, model, out_cols), BF16),
            dma((5,)),
            dma((2,)),
            dma((2, 2)),
            dma((2, 2)),
            dma((2, 2)),
            dma((2,)),
            dma((2,)),
            dma((2, groups)),
            dma((2, groups)),
            dma((1,)),
            dma((1,)),
            dma((2, 2)),
            dma((2, 2)),
            dma((2, 2)),
            dma((2, 2)),
        ],
        compiler_params=pltpu.CompilerParams(
            collective_id=4, has_side_effects=True, vmem_limit_bytes=63 * MIB
        ),
        cost_estimate=pl.CostEstimate(
            flops=8 * units * tokens * model,
            bytes_accessed=24 * MIB,
            transcendentals=2 * tokens * units,
        ),
        name="feed_forward_and_loss",
    )(
        info,
        seg_columns,
        gain,
        w_out,
        x_own,
        w_up,
        w_down,
        w_proj,
        o_t,
    )


def tail_kernel(
    dp_size,
    bucket_count,
    gain_ref,
    ffn_ref,
    last_ref,
    late_ref,
    pooled_ref,
    proj_ref,
    block_ref,
    act_ref,
    diag_ref,
    w_hbm,
    d_hbm,
    x_hbm,
    hidden_hbm,
    own_ref,
    chip_in,
    total_ref,
    g_qkv_ref,
    g_proj_ref,
    g_down_ref,
    w_ref,
    d_ref,
    x_ref,
    hidden_ref,
    near_out,
    near_in,
    part,
    gain_sum,
    chip_out,
    last_far,
    turned,
    seq_box,
    dp_box,
    load_sem,
    near_send,
    near_recv,
    chip_send,
    chip_recv,
    last_send,
    last_recv,
    seq_send,
    seq_recv,
    dp_send,
    dp_recv,
):
    seq_size = 4
    dp_at, seq_at = lax.axis_index("dp"), lax.axis_index("seq")
    row, turn = seq_at // 2, lax.rem(seq_at, 2)
    along_seq = lambda step: {"dp": dp_at, "seq": lax.rem(seq_at + step, seq_size)}
    along_dp = lambda step: {"dp": lax.rem(dp_at + step, dp_size), "seq": seq_at}
    other_core = {"dp": dp_at, "seq": row * 2 + 1 - turn}
    other_chip = {"dp": dp_at, "seq": lax.rem(seq_at + 2, seq_size)}
    model, piece = w_ref.shape[0], own_ref.shape[0]
    rows = g_proj_ref.shape[0]
    parts = TILE // BLOCK
    barrier = pltpu.get_barrier_semaphore()
    each(1, seq_size, lambda step: signal(barrier, along_seq(step)))
    each(1, dp_size, lambda step: signal(barrier, along_dp(step)))
    loads = [
        pltpu.make_async_copy(source, target, load_sem.at[at])
        for at, (source, target) in enumerate(
            [(w_hbm, w_ref), (d_hbm, d_ref), (x_hbm, x_ref), (hidden_hbm, hidden_ref)]
        )
    ]
    for load in loads:
        load.start()

    def product(member, at):
        which = jnp.where(at < 2, 1 - row, row)
        start = pl.multiple_of((member + 2 * which) * piece + lax.rem(at, 2) * TILE, TILE)
        return dot(w_ref[...], d_ref[:, pl.ds(start, TILE)])

    def near_copy(at):
        return remote(near_out.at[at], near_in.at[at], near_send.at[at], near_recv.at[at], other_core)

    def chip_copy(at):
        return remote(chip_out.at[at], chip_in.at[at], chip_send.at[at], chip_recv.at[at], other_chip)

    def last_copy(step, source):
        to = pl.ds(pl.multiple_of(lax.rem(dp_at + step, dp_size) * rows, rows), rows)
        return remote(
            last_ref.at[to, :], last_far.at[source], last_send.at[step], last_recv.at[source], along_dp(step)
        )

    gain_sum[...] = jnp.zeros_like(gain_sum)
    gain = gain_ref[...].reshape(1, model)
    loads[0].wait()
    loads[1].wait()
    def quarter(at):
        near_out[at] = product(1 - turn, at).astype(BF16)

        @pl.when(at == 0)
        def _():
            pl.semaphore_wait(barrier, seq_size - 1 + dp_size - 1)

        near_copy(at).start()
        part[...] = product(turn, at)

        @pl.when(at == 0)
        def _():
            each(1, dp_size, lambda step: last_copy(step, dp_at).start())
            loads[2].wait()
            loads[3].wait()

        near_copy(at).wait_recv()
        which = jnp.where(at < 2, 1 - row, row)

        def block(sub):
            lanes = pl.ds(pl.multiple_of(sub * BLOCK, BLOCK), BLOCK)
            place = pl.multiple_of(lax.rem(at, 2) * TILE + sub * BLOCK, BLOCK)
            there = pl.ds(pl.multiple_of(which * piece + place, BLOCK), BLOCK)
            grad = jnp.transpose(part[:, lanes] + near_in[at, :, lanes].astype(F32))
            x = x_ref[there, :].astype(F32)
            scale = lax.rsqrt(jnp.mean(x * x, axis=1, keepdims=True) + EPS)
            scaled = gain * grad
            inner = jnp.mean(scaled * x, axis=1, keepdims=True)
            gain_sum[...] += jnp.sum((grad * x * scale).reshape(BLOCK // 8, 8, model), axis=0)
            result = hidden_ref[there, :] + scale * scaled - x * (scale * scale * scale * inner)

            @pl.when(at < 2)
            def _():
                chip_out[at * parts + sub] = result.astype(BF16)
                chip_copy(at * parts + sub).start()

            @pl.when(at >= 2)
            def _():
                own_ref[pl.ds(place, BLOCK), :] = result

        each(0, parts, block)

    each(0, 4, quarter)

    heads = diag_ref.shape[0]
    sums = diag_ref[...].reshape(heads * 8, 2 * BLOCK)
    sums = [value.astype(BF16) for value in three_parts(sums)]
    row_at = lax.rem(lax.broadcasted_iota(jnp.int32, (heads * 8, 128), 0), 8)
    lane = lax.broadcasted_iota(jnp.int32, (2 * BLOCK, 128), 1)
    place = lax.broadcasted_iota(jnp.int32, (2 * BLOCK, 128), 0)
    place = jnp.where(place < BLOCK, place, place - 2 * BLOCK)
    table = jnp.zeros((heads * 8, 128), F32)
    for band in range(BANDS):
        offset = (band - BANDS // 2) * BLOCK - place
        onehot = jnp.where(bucket_of(offset, bucket_count // 2) == lane, 1.0, 0.0).astype(BF16)
        found = dot(sums[0], onehot) + dot(sums[1], onehot) + dot(sums[2], onehot)
        table = table + jnp.where(row_at == band, found, 0.0)
    table = jnp.sum(table.reshape(heads, 8, 128), axis=1)
    run = heads // 2
    table = jnp.concatenate(
        [
            jnp.where(
                (1 - row) * 2 + turn == group,
                table[:run],
                jnp.where(row * 2 + turn == group, table[run:], 0.0),
            )
            for group in range(4)
        ],
        axis=0,
    )

    def as_rows(value):
        value = jnp.sum(value, axis=0, keepdims=True)
        return [value[:, at : at + 128] for at in range(0, model, 128)]

    value = jnp.concatenate(as_rows(gain_sum[...]) + as_rows(ffn_ref[...]) + [table], axis=0)

    def stage_total(value, at, size, where, box, send, receive):
        box[at] = value
        copy = lambda step, source: remote(
            box.at[source], box.at[source], send.at[step], receive.at[source], where(step)
        )
        each(1, size, lambda step: copy(step, at).start())
        each(1, size, lambda step: copy(step, lax.rem(at + step, size)).wait_recv())
        total = box[0]
        for source in range(1, size):
            total = total + box[source]
        each(1, size, lambda step: copy(step, at).wait_send())
        return total

    value = stage_total(value, seq_at, seq_size, along_seq, seq_box, seq_send, seq_recv)
    total_ref[...] = stage_total(value, dp_at, dp_size, along_dp, dp_box, dp_send, dp_recv)

    own_rows = pl.ds(pl.multiple_of(dp_at * rows, rows), rows)
    out_cols = g_proj_ref.shape[1]
    own_cols = pl.ds(pl.multiple_of(seq_at * out_cols, out_cols), out_cols)
    turned[0] = jnp.transpose(pooled_ref[...].astype(F32))
    turned[1] = jnp.transpose(proj_ref[...].astype(F32))
    turned[2] = jnp.transpose(block_ref[...])
    g_proj_ref[...] = dot_nt(turned[0, own_rows, :].astype(BF16), turned[1, own_cols, :].astype(BF16))
    act = jnp.transpose(act_ref[...].reshape(pooled_ref.shape[0], act_ref.shape[2]))
    block = turned[2, own_cols, :].astype(BF16)
    high = act.astype(BF16)
    rest = (act - high.astype(F32)).astype(BF16)
    g_down_ref[...] = dot_nt(high, block) + dot_nt(rest, block)

    each(1, dp_size, lambda step: last_copy(step, lax.rem(dp_at + step, dp_size)).wait_recv())
    last_far[dp_at] = jnp.zeros(last_far.shape[1:], BF16)
    last = last_ref[own_rows, :].astype(F32)
    for source in range(dp_size):
        last = last + last_far[source].astype(F32)
    late = [late_ref[which] for which in range(late_ref.shape[0])] + [last]
    width = late_ref.shape[2] // 3
    for kind in range(3):
        g_qkv_ref[kind] = jnp.concatenate(
            [value[:, kind * width : (kind + 1) * width] for value in late], axis=1
        )
    for at in range(2 * parts):
        chip_copy(at).wait_recv()
    for at in range(4):
        near_copy(at).wait_send()
    for at in range(2 * parts):
        chip_copy(at).wait_send()
    each(1, dp_size, lambda step: last_copy(step, dp_at).wait_send())


def token_gradients(
    d_qkv, w_qkv, x_own, grad_hidden, gain, gain_ffn, last, late, pooled, proj, block, act, diag, buckets, dp_size
):
    tokens, model = x_own.shape
    piece, many = tokens // 2, pooled.shape[0]
    rows, out_cols = model // dp_size, model // 4
    run, width = late.shape[0] + 1, late.shape[2] // 3
    vmem, anywhere = pl.BlockSpec(memory_space=pltpu.VMEM), pl.BlockSpec(memory_space=pl.ANY)
    dma, shape = pltpu.SemaphoreType.DMA, jax.ShapeDtypeStruct
    return pl.pallas_call(
        functools.partial(tail_kernel, dp_size, buckets),
        in_specs=[vmem] * 9 + [anywhere] * 4,
        out_specs=[vmem] * 6,
        out_shape=[
            shape((piece, model), F32),
            shape((piece // BLOCK, BLOCK, model), BF16),
            shape((24, 128), F32),
            shape((3, rows, run * width), F32),
            shape((rows, out_cols), F32),
            shape((act.shape[2], out_cols), F32),
        ],
        scratch_shapes=[
            pltpu.VMEM(w_qkv.shape, BF16),
            pltpu.VMEM(d_qkv.shape, BF16),
            pltpu.VMEM(x_own.shape, BF16),
            pltpu.VMEM(grad_hidden.shape, F32),
            pltpu.VMEM((4, model, TILE), BF16),
            pltpu.VMEM((4, model, TILE), BF16),
            pltpu.VMEM((model, TILE), F32),
            pltpu.VMEM((8, model), F32),
            pltpu.VMEM((piece // BLOCK, BLOCK, model), BF16),
            pltpu.VMEM((dp_size, rows, last.shape[1]), BF16),
            pltpu.VMEM((3, model, many), F32),
            pltpu.VMEM((4, 24, 128), F32),
            pltpu.VMEM((dp_size, 24, 128), F32),
            dma((4,)),
            dma((4,)),
            dma((4,)),
            dma((piece // BLOCK,)),
            dma((piece // BLOCK,)),
            dma((dp_size,)),
            dma((dp_size,)),
            dma((4,)),
            dma((4,)),
            dma((dp_size,)),
            dma((dp_size,)),
        ],
        compiler_params=pltpu.CompilerParams(
            collective_id=3, has_side_effects=True, vmem_limit_bytes=63 * MIB
        ),
        cost_estimate=pl.CostEstimate(
            flops=2 * d_qkv.shape[0] * d_qkv.shape[1] * model,
            bytes_accessed=16 * MIB,
            transcendentals=0,
        ),
        name="token_gradients",
    )(
        gain,
        gain_ffn,
        last,
        late,
        pooled,
        proj,
        block,
        act,
        diag,
        w_qkv,
        d_qkv,
        x_own,
        grad_hidden,
    )


def normed(inputs, gain_vec):
    return inputs * lax.rsqrt(jnp.mean(inputs * inputs, axis=-1, keepdims=True) + EPS) * gain_vec


def norm_back(inputs, gain_vec, grads_in):
    scale = lax.rsqrt(jnp.mean(inputs * inputs, axis=-1, keepdims=True) + EPS)
    gain_grad = jnp.sum(grads_in * inputs * scale, axis=0)
    scaled = gain_vec * grads_in
    inner = jnp.mean(scaled * inputs, axis=-1, keepdims=True)
    return scale * scaled - inputs * (scale * scale * scale * inner), gain_grad


def on_device(
    tokens,
    segment_ids,
    pair_ids,
    w_query,
    w_key,
    w_value,
    w_out,
    w_up,
    w_down,
    w_proj,
    gain_attn,
    gain_ffn,
    rel_bias,
):
    _, piece, model_width = tokens.shape
    bucket_count, head_count = rel_bias.shape
    slots = pair_ids.shape[1]
    dp_size, seq_size = lax.axis_size("dp"), lax.axis_size("seq")
    half = seq_size // 2
    length = piece * seq_size
    heads = head_count // half
    width = model_width // head_count
    dp_at, seq_at = lax.axis_index("dp"), lax.axis_index("seq")
    row, turn = seq_at // half, lax.rem(seq_at, half)
    across = [(i, (i + half) % seq_size) for i in range(seq_size)]

    def by_row(own, other):
        return jnp.where(row == 0, own, other), jnp.where(row == 0, other, own)

    def among(step):
        return [(i, i // half * half + (i % half + step) % half) for i in range(seq_size)]

    def trade(own, send_to):
        entries = [own] * half
        for step in range(1, half):
            got = lax.ppermute(send_to(lax.rem(turn + step, half)), "seq", among(step))
            source = lax.rem(turn + half - step, half)
            entries = [jnp.where(source == j, got, entry) for j, entry in enumerate(entries)]
        return entries

    def pick(value, at, size, dim):
        return lax.dynamic_slice_in_dim(value, at * size, size, dim)

    def pieces_of(value, member, dim):
        return jnp.concatenate(
            [pick(value, member, piece, dim), pick(value, member + half, piece, dim)], axis=dim
        )

    def in_row_order(entries, dim):
        halves = [jnp.split(entry, 2, axis=dim) for entry in entries]
        return jnp.concatenate([pair[0] for pair in halves] + [pair[1] for pair in halves], axis=dim)

    def own_pieces(local):
        own = lax.dynamic_index_in_dim(local, row, 0, keepdims=False)
        other = lax.dynamic_index_in_dim(local, 1 - row, 0, keepdims=False)
        return jnp.concatenate(by_row(own, lax.ppermute(other, "seq", across)), axis=0)

    def whole_row(pair):
        return in_row_order(trade(pair, lambda member: pair), 0)

    def hand_back(pair, kind):
        own, other = pick(pair, row, piece, 0), pick(pair, 1 - row, piece, 0)
        return jnp.stack(by_row(own, lax.ppermute(other.astype(kind), "seq", across).astype(own.dtype)))

    aligned = seq_size == 4 and heads % 2 == 0
    blocks = 2 if aligned else 1
    block_heads = heads // blocks
    columns, block_columns = heads * width, block_heads * width

    def block_at(block):
        return (1 - row if block == 0 else row) if aligned else 0

    def cut(value, member, size, dim):
        parts = [pick(value, block_at(block) * half + member, size, dim) for block in range(blocks)]
        return jnp.concatenate(parts, axis=dim)

    if aligned:
        qkv_t, normed_t, x_pair, seg_row, w_own, info, seg_columns = gather_and_project(
            tokens, segment_ids, pair_ids, gain_attn, w_query, w_key, w_value, heads
        )
    else:
        x_pair, seg_own = own_pieces(tokens), own_pieces(segment_ids)
        x_row, seg_row = whole_row(x_pair), whole_row(seg_own)[None]
        w_qkv = [cut(weight, turn, block_columns, 1) for weight in (w_query, w_key, w_value)]
        w_qkv = [weight.reshape(model_width, heads, width) for weight in w_qkv]
        w_qkv = jnp.stack(w_qkv, axis=2).reshape(model_width, 3 * columns)
        normed_one = normed(x_row.astype(F32), gain_attn).astype(BF16)
        qkv_t = jnp.einsum("dc,td->ct", w_qkv, normed_one, preferred_element_type=F32).astype(BF16)
        x_own = x_pair.astype(F32)
        slot_ids = jnp.arange(slots, dtype=jnp.int32)
        counts = jnp.sum((seg_row == slot_ids[:, None]).astype(jnp.int32), axis=1)
        own_pairs = lax.dynamic_index_in_dim(pair_ids, row, 0, keepdims=False)
        info = jnp.stack([counts // 64, counts % 64, own_pairs], axis=1).astype(F32)
        info = jnp.concatenate([info, jnp.zeros((slots, 125), F32)], axis=1)
    qkv_t = qkv_t.reshape(heads, 3, width, length)
    table = cut(rel_bias, turn, block_heads, 1)
    onehot = (
        bucket_of(diagonal_offsets(), bucket_count // 2)[:, :, None]
        == jnp.arange(bucket_count, dtype=jnp.int32)
    ).astype(F32)
    diag = jnp.einsum("txb,bh->htx", onehot, table, precision=lax.Precision.HIGHEST)
    diag = jnp.concatenate([diag, jnp.zeros((heads, 8 - BANDS, 2 * BLOCK), F32)], axis=1)
    o_t, o_b, inverse, probs = attention_forward(slots, qkv_t, seg_row, diag)

    def heads_to_tokens(value):
        entries = trade(pieces_of(value, turn, 1), lambda member: pieces_of(value, member, 1))
        parts = [jnp.split(entry, blocks, axis=0) for entry in entries]
        if aligned:
            parts = [by_row(part[1], part[0]) for part in parts]
        return jnp.concatenate([part[block] for block in range(blocks) for part in parts], axis=0)

    def tokens_to_heads(value):
        own = cut(value, turn, block_columns, 0)
        return in_row_order(trade(own, lambda member: cut(value, member, block_columns, 0)), 1)

    if aligned:
        (
            mixed,
            loss,
            pooled,
            grad_proj,
            grad_block_all,
            every_act,
            g_t,
            grad_hidden,
            grad_gain_ffn,
            up_sum,
            out_sum,
        ) = feed_forward_and_loss(
            info,
            seg_columns,
            gain_ffn,
            w_out,
            x_pair,
            w_up,
            w_down,
            w_proj,
            o_b.reshape(columns, length),
            dp_size,
        )
        d_qkv, diag_grads, g_up, g_out, late, last = attention_backward_and_sums(
            qkv_t,
            g_t.reshape(heads, width, length),
            o_t,
            inverse,
            probs,
            normed_t,
            up_sum,
            out_sum,
            dp_size,
        )
        own, other, small, g_qkv, g_proj, g_down = token_gradients(
            d_qkv.reshape(-1, length),
            w_own,
            x_pair,
            grad_hidden,
            gain_attn,
            grad_gain_ffn,
            last,
            late,
            pooled,
            grad_proj,
            grad_block_all,
            every_act,
            diag_grads,
            bucket_count,
            dp_size,
        )
        g_query, g_key, g_value = g_qkv
        grad_tokens = jnp.stack(by_row(own, other.reshape(own.shape).astype(F32)))
        grad_gain_attn, grad_gain_ffn = small[:6].reshape(-1), small[6:12].reshape(-1)
        table_grad = small[12:, :bucket_count].T
    else:
        attended_t = heads_to_tokens(o_b.reshape(columns, length))
        hidden = x_own + jnp.einsum("ct,cd->td", attended_t, w_out, preferred_element_type=F32)
        normed_two = normed(hidden, gain_ffn).astype(BF16)
        up_proj = dot(normed_two, w_up)
        below = 0.5 * (1.0 + lax.erf(up_proj * (0.5**0.5)))
        act = (up_proj * below).astype(BF16)
        slope = (below + up_proj * jnp.exp(-0.5 * up_proj * up_proj) * 0.3989422804014327).astype(BF16)
        block_out = hidden + dot(act, w_down)
        mixed = hand_back(block_out.astype(BF16), BF16)
        member = (seg_own[None, :] == slot_ids[:, None]).astype(F32)
        sums = jnp.dot(member, block_out, precision=lax.Precision.HIGHEST)
        act_sums = dot(member.astype(BF16), act)

        loss, pooled, grad_proj, grad_block_all, every_act = loss_head(
            sums, act_sums, info, w_proj, dp_size, seq_size
        )
        grad_seg = lax.dynamic_slice_in_dim(grad_block_all, (dp_at * 2 + row) * slots, slots, 0)

        grad_act = dot_nt(grad_seg.astype(BF16), w_down)
        act_high = grad_act.astype(BF16)
        act_low = (grad_act - act_high.astype(F32)).astype(BF16)
        member_t = member.T.astype(BF16)
        spread = dot(
            jnp.concatenate([member_t, member_t], axis=1),
            jnp.concatenate([act_high, act_low], axis=0),
        )
        grad_up = (spread * slope.astype(F32)).astype(BF16)
        grad_wup = lax.dot_general(
            normed_two, grad_up, (((0,), (0,)), ((), ())), preferred_element_type=F32
        ).astype(BF16)
        grad_hidden, grad_gain_ffn = norm_back(hidden, gain_ffn, dot_nt(grad_up, w_up))
        grad_hidden = grad_hidden + jnp.dot(member.T, grad_seg, precision=lax.Precision.HIGHEST)
        grad_hidden_b = grad_hidden.astype(BF16)
        grad_wout = dot(attended_t, grad_hidden_b).astype(BF16)
        grad_att_t = dot_nt(w_out, grad_hidden_b).astype(BF16)
        g_t = tokens_to_heads(grad_att_t).reshape(heads, width, length)
        d_qkv, diag_grads = attention_backward(qkv_t, g_t, o_t, inverse, probs)
        every_act = every_act.reshape(-1, every_act.shape[2])
        proj_rows, proj_cols = model_width // dp_size, w_proj.shape[1] // seq_size
        g_proj = lax.dot_general(
            lax.dynamic_slice_in_dim(pooled, dp_at * proj_rows, proj_rows, 1),
            lax.dynamic_slice_in_dim(grad_proj, seq_at * proj_cols, proj_cols, 1),
            (((0,), (0,)), ((), ())),
            preferred_element_type=F32,
        )
        down_rows, down_cols = w_down.shape[0] // dp_size, model_width // seq_size
        g_down = lax.dot_general(
            every_act,
            lax.dynamic_slice_in_dim(grad_block_all, seq_at * down_cols, down_cols, 1)
            .astype(BF16)
            .astype(F32),
            (((0,), (0,)), ((), ())),
            precision=lax.Precision.HIGHEST,
        )
        table_part = jnp.einsum(
            "htx,txb->bh", diag_grads[:, :BANDS], onehot, precision=lax.Precision.HIGHEST
        )
        table_grad = jnp.zeros((bucket_count, head_count), F32)
        for block in range(blocks):
            table_grad = lax.dynamic_update_slice_in_dim(
                table_grad,
                table_part[:, block * block_heads : (block + 1) * block_heads],
                turn * block_heads,
                1,
            )
        def packed(gain_attn_part):
            small = jnp.concatenate([gain_attn_part, grad_gain_ffn, table_grad.reshape(-1)])
            return jnp.concatenate([small, jnp.zeros((-small.shape[0] % 1024,), F32)]).reshape(-1, 128)

        d_qkv = d_qkv.reshape(3 * columns, length)

        def owner_sum(value):
            value = lax.psum_scatter(value, "dp", scatter_dimension=0, tiled=True)
            return lax.psum_scatter(value, "seq", scatter_dimension=1, tiled=True).astype(F32)

        def own_columns(value):
            full = jnp.zeros((model_width, model_width), BF16)
            return lax.dynamic_update_slice_in_dim(full, value, turn * columns, 1)

        grad_w = lax.dot_general(
            normed_one, d_qkv, (((0,), (1,)), ((), ())), preferred_element_type=F32
        ).astype(BF16)
        grad_w = grad_w.reshape(model_width, heads, 3, width)
        g_query, g_key, g_value = [
            owner_sum(own_columns(grad_w[:, :, part].reshape(model_width, columns)))
            for part in range(3)
        ]
        g_up, g_out = owner_sum(grad_wup), owner_sum(grad_wout)
        grad_normed_part = jnp.einsum("ct,dc->td", d_qkv, w_qkv, preferred_element_type=F32)
        grad_normed = pieces_of(grad_normed_part, turn, 0)
        for step in range(1, half):
            send = pieces_of(grad_normed_part, lax.rem(turn + step, half), 0).astype(BF16)
            grad_normed = grad_normed + lax.ppermute(send, "seq", among(step)).astype(F32)
        grad_x, grad_gain_attn = norm_back(x_own, gain_attn, grad_normed)
        grad_tokens = hand_back(grad_hidden + grad_x, BF16)
        small = total_over_all(packed(grad_gain_attn), dp_size, seq_size)
        small = small.reshape(-1)
        grad_gain_attn, grad_gain_ffn = small[:model_width], small[model_width : 2 * model_width]
        table_grad = small[2 * model_width :][: bucket_count * head_count]
        table_grad = table_grad.reshape(bucket_count, head_count)
    return (
        mixed,
        loss[0, 0],
        grad_tokens,
        g_query,
        g_key,
        g_value,
        g_out,
        g_up,
        g_down,
        g_proj,
        grad_gain_attn,
        grad_gain_ffn,
        table_grad,
    )


def solution(mesh):
    in_specs = (P("dp", "seq", None), P("dp", "seq"), P("dp", None)) + (P(),) * 10
    out_specs = (
        (P("dp", "seq", None), P(), P("dp", "seq", None)) + (P("dp", "seq"),) * 7 + (P(),) * 3
    )
    return jax.shard_map(
        on_device, mesh=mesh, in_specs=in_specs, out_specs=out_specs, check_vma=False
    )
```

```python
import functools

import jax
import jax.numpy as jnp
from jax import lax
from jax.experimental import pallas as pl
from jax.experimental.pallas import tpu as pltpu
from jax.sharding import PartitionSpec as P

EPS = 1e-06
LOGIT_SCALE = 20.0
LIMITS = (12, 16, 23, 32, 46, 64, 91)
MASKED = -float(2**30)
TILE = 256
SPAN = 1024
BLOCK = 128
BANDS = 5
F32 = jnp.float32
BF16 = jnp.bfloat16
MIB = 1024 * 1024


def bucket_of(offset, half_count):
    distance = jnp.abs(offset)
    beyond = 8 + sum(((distance >= bound_at).astype(jnp.int32) for bound_at in LIMITS))
    nearby = jnp.where(distance < 8, distance, beyond)
    return nearby + half_count * (offset > 0).astype(jnp.int32)


def diagonal_offsets():
    diff = (jnp.arange(BANDS, dtype=jnp.int32) - BANDS // 2)[:, None] * BLOCK
    place = jnp.arange(2 * BLOCK, dtype=jnp.int32)[None, :]
    return diff - jnp.where(place < BLOCK, place, place - 2 * BLOCK)


def dot(left, right):
    return jnp.dot(left, right, preferred_element_type=F32)


def dot_nt(left, right):
    return lax.dot_general(left, right, (((1,), (1,)), ((), ())), preferred_element_type=F32)


def three_parts(value):
    high = value.astype(BF16).astype(F32)
    rest = value - high
    middle = rest.astype(BF16).astype(F32)
    return high, middle, rest - middle


def toeplitz(vector):
    rows, size = vector, 1
    while size < BLOCK:
        rows = jnp.concatenate([rows, pltpu.roll(rows, size, 1)], axis=0)
        size *= 2
    return rows[:, :BLOCK]


def diagonal_sums(block):
    rows, size = jnp.concatenate([block, jnp.zeros_like(block)], axis=1), BLOCK
    while size > 1:
        size //= 2
        rows = rows[:size] + pltpu.roll(rows[size:], 2 * BLOCK - size, 1)
    return rows


def blocks_of(band):
    for key in range(TILE // BLOCK):
        for query in range(TILE // BLOCK):
            apart = (band - BANDS // 2) * (TILE // BLOCK) + key - query
            row = min(max(apart, -(BANDS // 2)), BANDS // 2) + BANDS // 2
            yield pl.ds(key * BLOCK, BLOCK), pl.ds(query * BLOCK, BLOCK), row


def bias_tiles(diag_ref, bias):
    rows = [diag_ref[0, row : row + 1, :] for row in range(BANDS)]
    blocks = [toeplitz(row) for row in rows[1:-1]]
    blocks = [jnp.broadcast_to(rows[0][:, :BLOCK], (BLOCK, BLOCK))] + blocks
    blocks += [jnp.broadcast_to(rows[-1][:, :BLOCK], (BLOCK, BLOCK))]
    for band in range(BANDS):
        for keys, queries, row in blocks_of(band):
            bias[band, keys, queries] = blocks[row]


def segment_rows(seg, slots, inside, outside):
    iota = lax.broadcasted_iota(jnp.int32, (slots, seg.shape[1]), 0)
    return jnp.where(iota == seg, inside, outside).astype(F32)


def extended(head, seg_part, stat_rows):
    width = head.shape[1]
    stat = jnp.concatenate(
        list(stat_rows) + [jnp.zeros((8 - len(stat_rows), width), F32)], axis=0
    )
    more = jnp.concatenate([seg_part, stat], axis=0).astype(BF16)
    rest = jnp.zeros((128 - head.shape[0] - more.shape[0], width), BF16)
    return jnp.concatenate([head, more, rest], axis=0)


def keys_side(source_ref, seg_ref, target_ref, slots):
    length = source_ref.shape[3]
    for at in range(0, length, TILE):
        part = pl.ds(at, TILE)
        seg_part = segment_rows(seg_ref[0:1, part], slots, 1.0, 0.0)
        one = jnp.ones((1, TILE), F32)
        whole = extended(source_ref[0, 0, :, part], seg_part, [one, one, one])
        whole = jnp.transpose(whole.astype(F32)).astype(BF16)
        target_ref[part, :] = whole
        target_ref[pl.ds(length + at, TILE), :] = whole


def band_of(chunk, tile):
    return jnp.clip(chunk - tile, -(BANDS // 2), BANDS // 2) + BANDS // 2


def tile_part(tile):
    return pl.ds(pl.multiple_of(tile * TILE, TILE), TILE)


def chunk_at(tile, turn, count):
    return lax.rem(tile + turn, count)


def span_part(span, tile):
    return pl.ds(pl.multiple_of(tile * TILE, TILE) + span * SPAN, SPAN)


def is_far(turn, count):
    return 2 <= turn <= count - 2


def forward_kernel(
    slots, q_ref, k_ref, v_ref, seg_ref, diag_ref, o_ref, ob_ref, inv_ref, p_ref, kx, bias, held
):
    count, spans = k_ref.shape[3] // TILE, k_ref.shape[3] // SPAN
    keys_side(k_ref, seg_ref, kx, slots)
    bias_tiles(diag_ref, bias)
    before, after = diag_ref[0, 0:1, 0:1], diag_ref[0, BANDS - 1 : BANDS, 0:1]

    def query_side(tile):
        part = tile_part(tile)
        return extended(q_ref[0, 0, :, part], segment_rows(seg_ref[0:1, part], slots, 0.0, MASKED), [])

    def far_bias(chunk, tile):
        return jnp.where(chunk > tile, after, before)

    def score(span, tile, qx, top):
        products = dot(kx[span_part(span, tile), :], qx)
        for sub in range(SPAN // TILE):
            turn = span * (SPAN // TILE) + sub
            chunk = chunk_at(tile, turn, count)
            scores = products[sub * TILE : (sub + 1) * TILE]
            if not is_far(turn, count):
                scores = scores + bias[band_of(chunk, tile)]
            held[turn] = scores
            best = jnp.max(scores.reshape(TILE // 8, 8, TILE), axis=0)
            if is_far(turn, count):
                best = best + far_bias(chunk, tile)
            top = jnp.maximum(top, best)
        return top

    def weigh(turn, tile, top, out):
        chunk = chunk_at(tile, turn, count)
        shift = top - far_bias(chunk, tile) if is_far(turn, count) else top
        weights = jnp.exp(held[turn] - shift).astype(BF16)
        p_ref[0, tile_part(chunk), tile_part(tile)] = weights
        values = jnp.concatenate([v_ref[0, 0, :, tile_part(chunk)], jnp.ones((16, TILE), BF16)], axis=0)
        return out + dot(values, weights)

    def finish(tile, out):
        part = tile_part(tile)
        inverse = 1.0 / out[width : width + 1]
        out = out[:width] * inverse
        o_ref[0, :, part] = out
        ob_ref[0, :, part] = out.astype(BF16)
        inv_ref[0, :, part] = inverse

    width = v_ref.shape[2]
    lowest = jnp.full((8, TILE), -jnp.inf, F32)
    start = jnp.zeros((width + 16, TILE), F32)

    def body(tile, top):
        qx, following, out = query_side(tile + 1), lowest, start
        for span in range(spans):
            for turn in range(span * (SPAN // TILE), (span + 1) * (SPAN // TILE)):
                out = weigh(turn, tile, top, out)
            following = score(span, tile + 1, qx, following)
        finish(tile, out)
        return jnp.max(following, axis=0, keepdims=True)

    qx, top = query_side(0), lowest
    for span in range(spans):
        top = score(span, 0, qx, top)
    top = lax.fori_loop(0, count - 1, body, jnp.max(top, axis=0, keepdims=True))
    out = start
    for turn in range(count):
        out = weigh(turn, count - 1, top, out)
    finish(count - 1, out)


def head_spec(rows, length):
    return pl.BlockSpec((1, rows, length), lambda h: (h, 0, 0))


def part_spec(part, width, length):
    return pl.BlockSpec((1, 1, width, length), lambda h: (h, part, 0, 0))


def attention_forward(slots, qkv, seg_row, diag):
    heads, _, width, length = qkv.shape
    return pl.pallas_call(
        functools.partial(forward_kernel, slots),
        grid=(heads,),
        in_specs=[part_spec(part, width, length) for part in range(3)]
        + [pl.BlockSpec(seg_row.shape, lambda h: (0, 0)), head_spec(8, 2 * BLOCK)],
        out_specs=[
            head_spec(width, length),
            head_spec(width, length),
            head_spec(1, length),
            head_spec(length, length),
        ],
        out_shape=[
            jax.ShapeDtypeStruct((heads, width, length), F32),
            jax.ShapeDtypeStruct((heads, width, length), BF16),
            jax.ShapeDtypeStruct((heads, 1, length), F32),
            jax.ShapeDtypeStruct((heads, length, length), BF16),
        ],
        scratch_shapes=[
            pltpu.VMEM((2 * length, 128), BF16),
            pltpu.VMEM((BANDS, TILE, TILE), F32),
            pltpu.VMEM((length // TILE, TILE, TILE), F32),
        ],
        compiler_params=pltpu.CompilerParams(
            dimension_semantics=("arbitrary",), vmem_limit_bytes=56 * MIB
        ),
        cost_estimate=pl.CostEstimate(
            flops=heads * length * length * 512,
            bytes_accessed=heads * length * (width * 12 + length * 2),
            transcendentals=heads * length * length,
        ),
        name="attention_forward",
    )(qkv, qkv, qkv, seg_row, diag)


def remote(source, target, send, receive, where):
    return pltpu.make_async_remote_copy(
        src_ref=source,
        dst_ref=target,
        send_sem=send,
        recv_sem=receive,
        device_id=where,
        device_id_type=pl.DeviceIdType.MESH,
    )


def signal(barrier, where):
    pl.semaphore_signal(barrier, inc=1, device_id=where, device_id_type=pl.DeviceIdType.MESH)


def each(first, last, step):
    def body(index, carried):
        step(index)
        return carried

    lax.fori_loop(first, last, body, 0)


def head_backward(
    q_ref,
    k_ref,
    v_ref,
    g_ref,
    o_ref,
    inv_ref,
    p_ref,
    d_ref,
    dd_ref,
    vx,
    sums,
    far,
    dkv,
    gx,
    both,
    left,
    beside=None,
):
    width, length = k_ref.shape[2], k_ref.shape[3]
    count, subs = length // TILE, SPAN // TILE
    for at in range(0, length, TILE):
        part = pl.ds(at, TILE)
        ones = jnp.ones((8, TILE), BF16)
        rest = jnp.zeros((128 - width - 8, TILE), BF16)
        whole = jnp.concatenate([v_ref[0, 0, :, part], ones, rest], axis=0)
        whole = jnp.transpose(whole.astype(F32)).astype(BF16)
        vx[part, :] = whole
        vx[pl.ds(length + at, TILE), :] = whole
    sums[...] = jnp.zeros_like(sums)
    far[...] = jnp.zeros_like(far)
    dkv[...] = jnp.zeros_like(dkv)
    both[1] = jnp.zeros_like(both[1])
    left[1] = jnp.zeros_like(left[1])

    def queries_side(tile, slot):
        own = tile_part(tile)
        query, grad = q_ref[0, 0, :, own], g_ref[0, :, own].astype(F32)
        inverse = inv_ref[0, :, own]
        centre = jnp.sum(grad * o_ref[0, :, own], axis=0, keepdims=True) * inverse
        grad = (grad * inverse).astype(BF16)
        stats = jnp.concatenate(list(three_parts(-centre)) + [jnp.zeros((5, TILE), F32)], axis=0)
        gx[slot] = jnp.concatenate(
            [grad, stats.astype(BF16), jnp.zeros((128 - width - 8, TILE), BF16)], axis=0
        )
        nothing = jnp.zeros((width, TILE), F32)
        upper = jnp.transpose(jnp.concatenate([query.astype(F32), nothing], axis=0))
        lower = jnp.transpose(jnp.concatenate([nothing, grad.astype(F32)], axis=0))
        both[slot] = jnp.concatenate([upper, lower], axis=0).astype(BF16)

    def score(tile, span, slot):
        products = dot(vx[span_part(span, tile), :], gx[slot])
        for sub in range(subs):
            turn, rows = span * subs + sub, pl.ds(sub * TILE, TILE)
            chunk = chunk_at(tile, turn, count)
            weights = p_ref[0, tile_part(chunk), tile_part(tile)]
            grad_scores = weights * products[sub * TILE : (sub + 1) * TILE].astype(BF16)
            if not is_far(turn, count):
                sums[band_of(chunk, tile)] += grad_scores.astype(F32)
            left[span, rows, :TILE] = grad_scores
            left[span, rows, TILE:] = weights

    def gather(tile, span, slot, grad_query):
        products = dot(left[span], both[slot])
        row = lax.broadcasted_iota(jnp.int32, (16, TILE), 0)
        for sub in range(subs):
            turn = span * subs + sub
            chunk = chunk_at(tile, turn, count)
            part = tile_part(chunk)
            rows = slice(sub * TILE, (sub + 1) * TILE)
            dkv[part, :] += products[rows]
            marks = jnp.zeros((16, TILE), F32)
            if is_far(turn, count):
                marks = jnp.where(row == jnp.where(chunk > tile, 1, 0), 1.0, 0.0)
            keys = jnp.concatenate([k_ref[0, 0, :, part], marks.astype(BF16)], axis=0)
            grad_query = grad_query + dot(keys, left[span, rows, :TILE])
        return grad_query

    def store(tile, grad_query):
        d_ref[0, 0, :, tile_part(tile)] = grad_query[:width].astype(BF16)

    empty = jnp.zeros((width + 16, TILE), F32)

    def step(tile, slot, following, behind, grad_behind):
        score(tile, 0, slot)
        grad_behind = gather(behind, 1, 1 - slot, grad_behind)
        store(behind, grad_behind)
        far[...] += grad_behind[width : width + 8]
        queries_side(following, 1 - slot)
        score(tile, 1, slot)
        return gather(tile, 0, slot, empty)

    def one(tile, carried):
        if beside is not None:
            beside(tile)
        slot = lax.rem(tile, 2)
        return step(tile, slot, lax.rem(tile + 1, count), lax.rem(tile + count - 1, count), carried)

    queries_side(0, 0)
    carried = lax.fori_loop(0, count, one, empty)
    grad_last = gather(count - 1, 1, (count - 1) % 2, carried)
    store(count - 1, grad_last)
    far[...] += grad_last[width : width + 8]
    d_both = jnp.transpose(dkv[...])
    d_ref[0, 1] = d_both[:width].astype(BF16)
    d_ref[0, 2] = d_both[width:].astype(BF16)
    totals = [None] * BANDS
    for band in range(BANDS):
        for keys, queries, row in blocks_of(band):
            block = sums[band, keys, queries]
            if row in (0, BANDS - 1):
                block = jnp.sum(block.reshape(BLOCK // 8, 8, BLOCK), axis=0)
            totals[row] = block if totals[row] is None else totals[row] + block
    for row, total in enumerate(totals):
        if row in (0, BANDS - 1):
            more = far[min(row, 1) : min(row, 1) + 1, :]
            total = jnp.sum(total, axis=0, keepdims=True) + more[:, :BLOCK] + more[:, BLOCK:]
            total = jnp.concatenate([total, jnp.zeros_like(total)], axis=1)
        else:
            total = diagonal_sums(total)
        dd_ref[0, row : row + 1, :] = total
    dd_ref[0, BANDS:, :] = jnp.zeros((8 - BANDS, 2 * BLOCK), F32)


def added(left, right):
    return (left.astype(F32) + right.astype(F32)).astype(BF16)


def backward_kernel(
    dp_size,
    q_ref,
    k_ref,
    v_ref,
    g_ref,
    o_ref,
    inv_ref,
    p_ref,
    normed_ref,
    up_ref,
    out_ref,
    d_ref,
    dd_ref,
    g_up_ref,
    g_out_ref,
    g_late_ref,
    last_ref,
    vx,
    sums,
    far,
    dkv,
    gx,
    both,
    left,
    up_near,
    out_near,
    up_far,
    out_far,
    late_out,
    late_near,
    late_total,
    late_far,
    chip_send,
    chip_recv,
    late_send,
    late_recv,
    dp_send,
    dp_recv,
):
    head, heads = pl.program_id(0), pl.num_programs(0)
    own_heads = late_near.shape[0]
    dp_at, seq_at = lax.axis_index("dp"), lax.axis_index("seq")
    chip = seq_at // 2
    rows = g_up_ref.shape[0]
    other_chip = {"dp": dp_at, "seq": lax.rem(seq_at + 2, 4)}
    peer = lambda step: {"dp": lax.rem(dp_at + step, dp_size), "seq": seq_at}
    source_of = lambda step: lax.rem(dp_at + step, dp_size)
    rows_of = lambda which: pl.ds(pl.multiple_of(which * rows, rows), rows)

    def chip_copies():
        side, there = [up_ref.at[1 - chip], out_ref.at[1 - chip]], [up_near, out_near]
        return [
            remote(source, target, chip_send.at[at], chip_recv.at[at], other_chip)
            for at, (source, target) in enumerate(zip(side, there))
        ]

    def dp_copy(kind, step, source):
        to = rows_of(lax.rem(dp_at + step, dp_size))
        if kind == 0:
            item, there = up_near.at[to, :], up_far.at[source]
        elif kind == 1:
            item, there = out_near.at[to, :], out_far.at[source]
        else:
            item, there = late_total.at[kind - 2, to, :], late_far.at[kind - 2, source]
        return remote(item, there, dp_send.at[kind, step], dp_recv.at[kind, source], peer(step))

    def late_copy(which):
        return remote(
            late_out.at[which], late_near.at[which], late_send.at[which], late_recv.at[which], other_chip
        )

    @pl.when(head == 0)
    def _():
        barrier = pltpu.get_barrier_semaphore()
        signal(barrier, other_chip)
        each(1, dp_size, lambda step: signal(barrier, peer(step)))
        pl.semaphore_wait(barrier, dp_size)
        for copy in chip_copies():
            copy.start()

    def beside(index):
        @pl.when((head == own_heads - 1) & (index == 2))
        def _():
            for copy in chip_copies():
                copy.wait_recv()

            def body(block):
                part = rows_of(block)
                up_near[part, :] = added(up_ref[chip, part, :], up_near[part, :])
                out_near[part, :] = added(out_ref[chip, part, :], out_near[part, :])

            each(0, dp_size, body)
            for kind in range(2):
                each(1, dp_size, lambda step: dp_copy(kind, step, dp_at).start())

    head_backward(
        q_ref,
        k_ref,
        v_ref,
        g_ref,
        o_ref,
        inv_ref,
        p_ref,
        d_ref,
        dd_ref,
        vx,
        sums,
        far,
        dkv,
        gx,
        both,
        left,
        beside,
    )
    grad_w = dot_nt(normed_ref[...], d_ref[0].reshape(-1, d_ref.shape[3]))

    @pl.when(head < own_heads)
    def _():
        late_out[head] = grad_w.astype(BF16)
        late_copy(head).start()

    for which in range(own_heads):

        @pl.when(head == own_heads + which)
        def _():
            late_copy(which).wait_recv()
            both = (grad_w + late_near[which].astype(F32)).astype(BF16)
            if which == own_heads - 1:
                last_ref[...] = both
            else:
                late_total[which] = both
                each(1, dp_size, lambda step: dp_copy(2 + which, step, dp_at).start())

    @pl.when(head == heads - 1)
    def _():
        for copy in chip_copies() + [late_copy(which) for which in range(own_heads)]:
            copy.wait_send()
        mine = rows_of(dp_at)
        totals = [
            up_near[mine, :].astype(F32),
            out_near[mine, :].astype(F32),
        ] + [late_total[which, mine, :].astype(F32) for which in range(own_heads - 1)]
        boxes = [up_far, out_far] + [late_far.at[which] for which in range(own_heads - 1)]
        for kind, box in enumerate(boxes):
            each(1, dp_size, lambda step: dp_copy(kind, step, source_of(step)).wait_recv())
            box[dp_at] = jnp.zeros(box.shape[1:], BF16)
            for source in range(dp_size):
                totals[kind] = totals[kind] + box[source].astype(F32)
            each(1, dp_size, lambda step: dp_copy(kind, step, dp_at).wait_send())
        g_up_ref[...] = totals[0]
        g_out_ref[...] = totals[1]
        for which in range(own_heads - 1):
            g_late_ref[which] = totals[2 + which]


def backward_specs(heads, width, length):
    specs = dict(
        in_specs=[part_spec(part, width, length) for part in range(3)]
        + [
            head_spec(width, length),
            head_spec(width, length),
            head_spec(1, length),
            head_spec(length, length),
        ],
        out_specs=[
            pl.BlockSpec((1, 3, width, length), lambda h: (h, 0, 0, 0)),
            head_spec(8, 2 * BLOCK),
        ],
        out_shape=[
            jax.ShapeDtypeStruct((heads, 3, width, length), BF16),
            jax.ShapeDtypeStruct((heads, 8, 2 * BLOCK), F32),
        ],
        scratch_shapes=[
            pltpu.VMEM((2 * length, 128), BF16),
            pltpu.VMEM((BANDS, TILE, TILE), F32),
            pltpu.VMEM((8, TILE), F32),
            pltpu.VMEM((length, 128), F32),
            pltpu.VMEM((2, 128, TILE), BF16),
            pltpu.VMEM((2, 2 * TILE, 128), BF16),
            pltpu.VMEM((2, SPAN, 2 * TILE), BF16),
        ],
    )
    cost = pl.CostEstimate(
        flops=heads * length * length * 1024,
        bytes_accessed=heads * length * (width * 20 + length * 2),
        transcendentals=0,
    )
    return specs, cost


def attention_backward(qkv, g_t, o_t, inverse, probs):
    heads, _, width, length = qkv.shape
    specs, cost = backward_specs(heads, width, length)
    return pl.pallas_call(
        head_backward,
        grid=(heads,),
        compiler_params=pltpu.CompilerParams(
            dimension_semantics=("arbitrary",), vmem_limit_bytes=56 * MIB
        ),
        cost_estimate=cost,
        name="attention_backward",
        **specs,
    )(qkv, qkv, qkv, g_t, o_t, inverse, probs)


def attention_backward_and_sums(
    qkv, g_t, o_t, inverse, probs, normed_t, up_sum, out_sum, dp_size
):
    heads, _, width, length = qkv.shape
    specs, cost = backward_specs(heads, width, length)
    own_heads = heads // 2
    _, model, cols = up_sum.shape
    out_cols = out_sum.shape[2]
    rows, late = model // dp_size, 3 * width
    vmem = pl.BlockSpec(memory_space=pltpu.VMEM)
    dma = pltpu.SemaphoreType.DMA
    specs["in_specs"] += [vmem] * 3
    specs["out_specs"] += [vmem] * 4
    specs["out_shape"] += [
        jax.ShapeDtypeStruct((rows, cols), F32),
        jax.ShapeDtypeStruct((rows, out_cols), F32),
        jax.ShapeDtypeStruct((own_heads - 1, rows, late), F32),
        jax.ShapeDtypeStruct((model, late), BF16),
    ]
    specs["scratch_shapes"] += [
        pltpu.VMEM((model, cols), BF16),
        pltpu.VMEM((model, out_cols), BF16),
        pltpu.VMEM((dp_size, rows, cols), BF16),
        pltpu.VMEM((dp_size, rows, out_cols), BF16),
        pltpu.VMEM((own_heads, model, late), BF16),
        pltpu.VMEM((own_heads, model, late), BF16),
        pltpu.VMEM((own_heads - 1, model, late), BF16),
        pltpu.VMEM((own_heads - 1, dp_size, rows, late), BF16),
        dma((2,)),
        dma((2,)),
        dma((own_heads,)),
        dma((own_heads,)),
        dma((1 + own_heads, dp_size)),
        dma((1 + own_heads, dp_size)),
    ]
    return pl.pallas_call(
        functools.partial(backward_kernel, dp_size),
        grid=(heads,),
        compiler_params=pltpu.CompilerParams(
            dimension_semantics=("arbitrary",),
            vmem_limit_bytes=60 * MIB,
            collective_id=2,
            has_side_effects=True,
        ),
        cost_estimate=cost,
        name="attention_backward_and_sums",
        **specs,
    )(qkv, qkv, qkv, g_t, o_t, inverse, probs, normed_t, up_sum, out_sum)


def loss_terms(inbox, w_ref, slots, loss_ref, pooled_ref, grad_proj_ref, grad_block_ref):
    groups, _, lanes = inbox.shape
    model = 2 * (lanes - 128)
    every = inbox[...].astype(F32)
    many = groups * slots
    flat = lambda value: value.reshape(many, value.shape[2])
    pooled = jnp.concatenate(
        [flat(every[:, :slots, : model // 2]), flat(every[:, slots:, : model // 2])], axis=1
    ).astype(BF16)
    info = flat(every[:, :slots, model // 2 :])
    counts = info[:, 0:1] * 64.0 + info[:, 1:2]
    proj = dot(pooled, w_ref[...])
    inverse = lax.rsqrt(jnp.sum(proj * proj, axis=-1, keepdims=True) + EPS)
    embed = (proj * inverse).astype(BF16)
    logits = LOGIT_SCALE * dot_nt(embed, embed)
    rows_at = lax.broadcasted_iota(jnp.int32, (many, many), 0)
    self_mask = rows_at == lax.broadcasted_iota(jnp.int32, (many, many), 1)
    pairs = jnp.broadcast_to(info[:, 2:3], (many, many))
    partner = jnp.where(self_mask, 0.0, jnp.where(pairs == jnp.transpose(pairs), 1.0, 0.0))
    masked = jnp.where(self_mask, -1000000000.0, logits)
    top = jnp.max(masked, axis=-1, keepdims=True)
    log_total = top + jnp.log(jnp.sum(jnp.exp(masked - top), axis=-1, keepdims=True))
    positive = jnp.sum(jnp.where(partner > 0.0, logits, 0.0), axis=-1, keepdims=True)
    loss = jnp.sum(log_total - positive, axis=0, keepdims=True) / many
    loss_ref[...] = jnp.broadcast_to(loss, loss_ref.shape)
    grad_raw = LOGIT_SCALE * ((jnp.exp(masked - log_total) - partner) / many)
    grad_raw = grad_raw.astype(BF16)
    turned = jnp.transpose(grad_raw.astype(F32)).astype(BF16)
    grad_embed = dot(grad_raw, embed) + dot(turned, embed)
    inner = jnp.sum(proj * grad_embed, axis=-1, keepdims=True)
    grad_proj = inverse * grad_embed - inverse * inverse * inverse * proj * inner
    grad_proj = grad_proj.astype(BF16)
    pooled_ref[...] = pooled
    grad_proj_ref[...] = grad_proj
    grad_block_ref[...] = dot_nt(grad_proj, w_ref[...]) / counts


def head_kernel(
    dp_size,
    seq_size,
    sums_ref,
    act_ref,
    info_ref,
    w_ref,
    loss_ref,
    pooled_ref,
    grad_proj_ref,
    grad_block_ref,
    act_all_ref,
    near_sums,
    near_act,
    act_total,
    inbox,
    act_inbox,
    near_send,
    near_recv,
    far_send,
    far_recv,
):
    half, groups = seq_size // 2, 2 * dp_size
    dp_at, seq_at = lax.axis_index("dp"), lax.axis_index("seq")
    row, turn = seq_at // half, lax.rem(seq_at, half)
    me = dp_at * 2 + row
    model = sums_ref.shape[1]
    slots = sums_ref.shape[0]

    def member(step):
        return lax.rem(turn + step, half)

    def sibling(step):
        return {"dp": dp_at, "seq": row * half + member(step)}

    def group(step):
        return lax.rem(me + step, groups)

    def peer(step):
        other = group(step)
        return {"dp": other // 2, "seq": lax.rem(other, 2) * half + turn}

    barrier = pltpu.get_barrier_semaphore()
    for step in range(1, half):
        signal(barrier, sibling(step))
    each(1, groups, lambda step: signal(barrier, peer(step)))
    near_sums[turn] = sums_ref[...]
    near_act[turn] = act_ref[...]
    pl.semaphore_wait(barrier, half - 1 + groups - 1)

    def near(step, source):
        return [
            remote(
                buffer.at[source],
                buffer.at[source],
                near_send.at[kind, step],
                near_recv.at[kind, source],
                sibling(step),
            )
            for kind, buffer in enumerate((near_sums, near_act))
        ]

    for step in range(1, half):
        for copy in near(step, turn):
            copy.start()
    for step in range(1, half):
        for copy in near(step, member(step)):
            copy.wait_recv()
    sums, act = near_sums[0], near_act[0]
    for source in range(1, half):
        sums, act = sums + near_sums[source], act + near_act[source]
    info = info_ref[...]
    pooled = sums / (info[:, 0:1] * 64.0 + info[:, 1:2])
    inbox[me] = jnp.concatenate(
        [
            jnp.concatenate([pooled[:, : model // 2], info], axis=1),
            jnp.concatenate([pooled[:, model // 2 :], jnp.zeros_like(info)], axis=1),
        ],
        axis=0,
    ).astype(BF16)
    act_total[...] = act
    act_inbox[me] = act_total[dp_at]

    def message(step, source):
        return remote(
            inbox.at[source], inbox.at[source], far_send.at[0, step], far_recv.at[0, source], peer(step)
        )

    def act_message(step, source):
        return remote(
            act_total.at[group(step) // 2],
            act_inbox.at[source],
            far_send.at[1, step],
            far_recv.at[1, source],
            peer(step),
        )

    each(1, groups, lambda step: message(step, me).start())
    each(1, groups, lambda step: act_message(step, me).start())
    each(1, groups, lambda step: message(step, group(step)).wait_recv())

    loss_terms(inbox, w_ref, slots, loss_ref, pooled_ref, grad_proj_ref, grad_block_ref)
    each(1, groups, lambda step: act_message(step, group(step)).wait_recv())
    act_all_ref[...] = act_inbox[...]
    for step in range(1, half):
        for copy in near(step, turn):
            copy.wait_send()
    each(1, groups, lambda step: message(step, me).wait_send())
    each(1, groups, lambda step: act_message(step, me).wait_send())


def loss_head(sums, act_sums, info, w_proj, dp_size, seq_size):
    slots, model = sums.shape
    groups, half, many = 2 * dp_size, seq_size // 2, 2 * dp_size * slots
    cols = act_sums.shape[1] // dp_size
    act_parts = act_sums.reshape(slots, dp_size, cols).transpose(1, 0, 2)
    vmem = pl.BlockSpec(memory_space=pltpu.VMEM)
    return pl.pallas_call(
        functools.partial(head_kernel, dp_size, seq_size),
        in_specs=[vmem] * 4,
        out_specs=[vmem] * 5,
        out_shape=[
            jax.ShapeDtypeStruct((8, 128), F32),
            jax.ShapeDtypeStruct((many, model), BF16),
            jax.ShapeDtypeStruct((many, w_proj.shape[1]), BF16),
            jax.ShapeDtypeStruct((many, model), F32),
            jax.ShapeDtypeStruct((groups, slots, cols), F32),
        ],
        scratch_shapes=[
            pltpu.VMEM((half, slots, model), F32),
            pltpu.VMEM((half, dp_size, slots, cols), F32),
            pltpu.VMEM((dp_size, slots, cols), F32),
            pltpu.VMEM((groups, 2 * slots, model // 2 + 128), BF16),
            pltpu.VMEM((groups, slots, cols), F32),
            pltpu.SemaphoreType.DMA((2, half)),
            pltpu.SemaphoreType.DMA((2, half)),
            pltpu.SemaphoreType.DMA((2, groups)),
            pltpu.SemaphoreType.DMA((2, groups)),
        ],
        compiler_params=pltpu.CompilerParams(
            collective_id=0, has_side_effects=True, vmem_limit_bytes=40 * MIB
        ),
        cost_estimate=pl.CostEstimate(
            flops=4 * many * model * model, bytes_accessed=8 * MIB, transcendentals=many * many
        ),
        name="loss_head",
    )(sums, act_parts, info, w_proj)


def total_kernel(
    dp_size, seq_size, value_ref, out_ref, seq_box, dp_box, seq_send, seq_recv, dp_send, dp_recv
):
    dp_at, seq_at = lax.axis_index("dp"), lax.axis_index("seq")
    along_seq = lambda step: {"dp": dp_at, "seq": lax.rem(seq_at + step, seq_size)}
    along_dp = lambda step: {"dp": lax.rem(dp_at + step, dp_size), "seq": seq_at}
    barrier = pltpu.get_barrier_semaphore()
    each(1, seq_size, lambda step: signal(barrier, along_seq(step)))
    each(1, dp_size, lambda step: signal(barrier, along_dp(step)))
    pl.semaphore_wait(barrier, seq_size - 1 + dp_size - 1)

    def stage(value, at, size, where, box, send, receive):
        box[at] = value
        copy = lambda step, source: remote(
            box.at[source], box.at[source], send.at[step], receive.at[source], where(step)
        )
        each(1, size, lambda step: copy(step, at).start())
        each(1, size, lambda step: copy(step, lax.rem(at + step, size)).wait_recv())
        total = box[0]
        for source in range(1, size):
            total = total + box[source]
        each(1, size, lambda step: copy(step, at).wait_send())
        return total

    value = stage(value_ref[...], seq_at, seq_size, along_seq, seq_box, seq_send, seq_recv)
    out_ref[...] = stage(value, dp_at, dp_size, along_dp, dp_box, dp_send, dp_recv)


def total_over_all(value, dp_size, seq_size):
    vmem = pl.BlockSpec(memory_space=pltpu.VMEM)
    return pl.pallas_call(
        functools.partial(total_kernel, dp_size, seq_size),
        in_specs=[vmem],
        out_specs=vmem,
        out_shape=jax.ShapeDtypeStruct(value.shape, F32),
        scratch_shapes=[
            pltpu.VMEM((seq_size,) + value.shape, F32),
            pltpu.VMEM((dp_size,) + value.shape, F32),
            pltpu.SemaphoreType.DMA((seq_size,)),
            pltpu.SemaphoreType.DMA((seq_size,)),
            pltpu.SemaphoreType.DMA((dp_size,)),
            pltpu.SemaphoreType.DMA((dp_size,)),
        ],
        compiler_params=pltpu.CompilerParams(collective_id=1, has_side_effects=True),
        name="total_over_all",
    )(value)


def front_kernel(
    tokens_ref,
    seg_ref,
    pair_ref,
    gain_ref,
    wq_hbm,
    wk_hbm,
    wv_hbm,
    qkv_hbm,
    normed_hbm,
    own_hbm,
    row_ref,
    w_own_hbm,
    info_ref,
    column_ref,
    qkv_ref,
    normed_ref,
    w_own_ref,
    x_all,
    seg_here,
    seg_all,
    weights,
    turned,
    w_t,
    load_sem,
    store_sem,
    x_send,
    x_recv,
    seg_send,
    seg_recv,
):
    seq_at = lax.axis_index("seq")
    dp_at = lax.axis_index("dp")
    row, turn = seq_at // 2, lax.rem(seq_at, 2)
    other_core = {"dp": dp_at, "seq": row * 2 + 1 - turn}
    other_chip = {"dp": dp_at, "seq": lax.rem(seq_at + 2, 4)}
    piece, model = x_all.shape[1:]
    width = 64
    halves = piece // TILE
    heads = w_t.shape[0] // (3 * width)
    block_cols = heads // 2 * width
    loads = [
        pltpu.make_async_copy(source, weights.at[at], load_sem.at[at])
        for at, source in enumerate((wq_hbm, wk_hbm, wv_hbm))
    ]
    barrier = pltpu.get_barrier_semaphore()
    signal(barrier, other_core)
    signal(barrier, other_chip)
    for load in loads:
        load.start()
    for at in range(2):
        seg_here[at] = jnp.broadcast_to(seg_ref[at : at + 1, :], seg_here.shape[1:])
    pl.semaphore_wait(barrier, 2)

    def part_of(half):
        return tile_part(half)

    def chip_copy(half, slot):
        return remote(
            tokens_ref.at[1 - row, part_of(half), :],
            x_all.at[slot, part_of(half), :],
            x_send.at[0, half],
            x_recv.at[0, half],
            other_chip,
        )

    def core_copy(kind, half, slot):
        source = tokens_ref.at[row, part_of(half), :] if kind == 1 else x_all.at[slot, part_of(half), :]
        return remote(
            source,
            x_all.at[slot, part_of(half), :],
            x_send.at[kind, half],
            x_recv.at[kind, half],
            other_core,
        )

    def seg_copy(kind, slot):
        source = [seg_here.at[1 - row], seg_here.at[row], seg_all.at[slot]][kind]
        where = other_chip if kind == 0 else other_core
        return remote(source, seg_all.at[slot], seg_send.at[kind], seg_recv.at[kind], where)

    mine, partner = seq_at, lax.rem(seq_at + 2, 4)
    beside, beyond = row * 2 + 1 - turn, lax.rem(row * 2 + 1 - turn + 2, 4)
    for half in range(halves):
        chip_copy(half, mine).start()
    for half in range(halves):
        core_copy(1, half, mine).start()
    seg_copy(0, mine).start()
    seg_copy(1, mine).start()
    x_all[mine] = tokens_ref[row]
    seg_all[mine] = seg_here[row]

    for load in loads:
        load.wait()
    for at in range(3):

        def turn_strip(strip):
            part = tile_part(strip)
            turned[part, :] = jnp.transpose(weights[at, :, part].astype(F32)).astype(BF16)

        each(0, model // TILE, turn_strip)
        for head in range(heads):
            block = head // (heads // 2)
            which = 1 - row if block == 0 else row
            start = pl.multiple_of((which * 2 + turn) * block_cols, block_cols)
            start = start + head % (heads // 2) * width
            w_t[pl.ds((head * 3 + at) * width, width), :] = turned[pl.ds(start, width), :]
    gain = gain_ref[...].reshape(1, model)

    def project(slot, half):
        part = tile_part(half)
        x = x_all[slot, part, :].astype(F32)
        scale = lax.rsqrt(jnp.mean(x * x, axis=1, keepdims=True) + EPS)
        normed_part = jnp.transpose(x * scale * gain).astype(BF16)
        lanes = pl.ds(pl.multiple_of(slot * piece + half * TILE, TILE), TILE)
        normed_ref[:, lanes] = normed_part
        qkv_ref[:, lanes] = dot(w_t[...], normed_part).astype(BF16)

    def results(slot, at):
        lanes = pl.ds(pl.multiple_of(slot * piece, piece), piece)
        return [
            pltpu.make_async_copy(source.at[:, lanes], target.at[:, lanes], store_sem.at[kind, at])
            for kind, (source, target) in enumerate([(qkv_ref, qkv_hbm), (normed_ref, normed_hbm)])
        ]

    order = (mine, beside, partner, beyond)
    own_copies = [
        pltpu.make_async_copy(
            x_all.at[turn + 2 * which], own_hbm.at[pl.ds(which * piece, piece), :], store_sem.at[2, which]
        )
        for which in range(2)
    ] + [pltpu.make_async_copy(w_own_ref, w_own_hbm, store_sem.at[2, 2])]

    def unit(at):
        which, half = at // halves, lax.rem(at, halves)
        slot = jnp.where(which == 0, mine, jnp.where(which == 1, beside, jnp.where(which == 2, partner, beyond)))

        @pl.when(which == 1)
        def _():
            core_copy(1, half, beside).wait_recv()

        @pl.when(at == 2 * halves)
        def _():
            def turn_back(strip):
                part = pl.ds(pl.multiple_of(strip * BLOCK, BLOCK), BLOCK)
                w_own_ref[:, part] = jnp.transpose(w_t[part, :].astype(F32)).astype(BF16)

            each(0, w_t.shape[0] // BLOCK, turn_back)
            own_copies[2].start()
            seg_copy(0, partner).wait_recv()
            seg_copy(2, partner).start()

        @pl.when(which == 2)
        def _():
            chip_copy(half, partner).wait_recv()
            core_copy(2, half, partner).start()

        @pl.when(which == 3)
        def _():
            core_copy(2, half, beyond).wait_recv()

        project(slot, half)

        @pl.when(half == halves - 1)
        def _():
            for copy in results(slot, which):
                copy.start()

    each(0, 4 * halves, unit)
    for copy in own_copies[:2]:
        copy.start()
    seg_copy(1, beside).wait_recv()
    seg_copy(2, beyond).wait_recv()
    slots = info_ref.shape[0]
    ids = lax.broadcasted_iota(jnp.int32, (slots, piece), 0)
    counts = jnp.zeros((slots, 1), F32)
    for slot in range(4):
        row_ref[:, pl.ds(slot * piece, piece)] = seg_all[slot]
        hit = jnp.where(seg_all[slot] == ids, 1.0, 0.0)
        counts = counts + jnp.sum(hit, axis=1, keepdims=True)
    for which in range(2):
        column = jnp.transpose(jnp.broadcast_to(seg_all[turn + 2 * which, 0:1, :].astype(F32), (128, piece)))
        column_ref[pl.ds(which * piece, piece), :] = column.astype(jnp.int32)
    lane = lax.broadcasted_iota(jnp.int32, info_ref.shape, 1)
    own_pairs = jnp.broadcast_to(pair_ref[pl.ds(row, 1), :].astype(F32), (slots, slots))
    square = lax.broadcasted_iota(jnp.int32, (slots, slots), 0)
    square = square == lax.broadcasted_iota(jnp.int32, (slots, slots), 1)
    own_pairs = jnp.sum(jnp.where(square, own_pairs, 0.0), axis=1, keepdims=True)
    high = jnp.floor(counts * (1.0 / 64.0))
    info = jnp.where(lane == 0, high, jnp.where(lane == 1, counts - 64.0 * high, 0.0))
    info_ref[...] = jnp.where(lane == 2, own_pairs, info)
    for half in range(halves):
        chip_copy(half, mine).wait_send()
        core_copy(1, half, mine).wait_send()
        core_copy(2, half, partner).wait_send()
    for kind, slot in enumerate((mine, mine, partner)):
        seg_copy(kind, slot).wait_send()
    for copy in own_copies + [copy for at, slot in enumerate(order) for copy in results(slot, at)]:
        copy.wait()


def gather_and_project(tokens, segment_ids, pair_ids, gain, w_query, w_key, w_value, heads):
    _, piece, model = tokens.shape
    columns, length = 3 * heads * 64, 4 * piece
    vmem, anywhere = pl.BlockSpec(memory_space=pltpu.VMEM), pl.BlockSpec(memory_space=pl.ANY)
    dma = pltpu.SemaphoreType.DMA
    return pl.pallas_call(
        front_kernel,
        in_specs=[vmem] * 4 + [anywhere] * 3,
        out_specs=[anywhere] * 3 + [vmem, anywhere, vmem, vmem],
        out_shape=[
            jax.ShapeDtypeStruct((columns, length), BF16),
            jax.ShapeDtypeStruct((model, length), BF16),
            jax.ShapeDtypeStruct((2 * piece, model), BF16),
            jax.ShapeDtypeStruct((8, length), jnp.int32),
            jax.ShapeDtypeStruct((model, columns), BF16),
            jax.ShapeDtypeStruct((pair_ids.shape[1], 128), F32),
            jax.ShapeDtypeStruct((2 * piece, 128), jnp.int32),
        ],
        scratch_shapes=[
            pltpu.VMEM((columns, length), BF16),
            pltpu.VMEM((model, length), BF16),
            pltpu.VMEM((model, columns), BF16),
            pltpu.VMEM((4, piece, model), BF16),
            pltpu.VMEM((2, 8, piece), jnp.int32),
            pltpu.VMEM((4, 8, piece), jnp.int32),
            pltpu.VMEM((3, model, model), BF16),
            pltpu.VMEM((model, model), BF16),
            pltpu.VMEM((columns, model), BF16),
            dma((3,)),
            dma((3, 4)),
            dma((3, piece // TILE)),
            dma((3, piece // TILE)),
            dma((3,)),
            dma((3,)),
        ],
        compiler_params=pltpu.CompilerParams(
            collective_id=5, has_side_effects=True, vmem_limit_bytes=63 * MIB
        ),
        cost_estimate=pl.CostEstimate(
            flops=2 * columns * length * model, bytes_accessed=20 * MIB, transcendentals=0
        ),
        name="gather_and_project",
    )(
        tokens,
        segment_ids,
        pair_ids,
        gain,
        w_query,
        w_key,
        w_value,
    )


def middle_kernel(
    dp_size,
    info_ref,
    seg_ref,
    gain_ref,
    w_out_hbm,
    x_hbm,
    w_up_hbm,
    w_down_hbm,
    w_proj_hbm,
    o_hbm,
    mixed_ref,
    loss_ref,
    pooled_ref,
    grad_proj_ref,
    grad_block_ref,
    act_all_ref,
    g_ref,
    grad_hbm,
    gain_sum,
    up_ref,
    out_ref,
    w_out,
    x_own,
    w_up,
    w_down,
    w_proj,
    attended,
    hidden,
    normed_two,
    normed_t,
    act,
    slope,
    total,
    raw,
    members_t,
    sum_parts,
    mixed_out,
    near_sums,
    near_act,
    act_total,
    inbox,
    act_inbox,
    grad_b,
    grad_att,
    out_send,
    out_recv,
    load_sem,
    store_sem,
    head_load,
    head_send,
    head_recv,
    near_send,
    near_recv,
    far_send,
    far_recv,
    mixed_send,
    mixed_recv,
    att_send,
    att_recv,
    core_send,
    core_recv,
):
    dp_at, seq_at = lax.axis_index("dp"), lax.axis_index("seq")
    row, turn = seq_at // 2, lax.rem(seq_at, 2)
    groups, me = 2 * dp_size, dp_at * 2 + row
    other_core = {"dp": dp_at, "seq": row * 2 + 1 - turn}
    other_chip = {"dp": dp_at, "seq": lax.rem(seq_at + 2, 4)}
    group = lambda step: lax.rem(me + step, groups)
    peer = lambda step: {"dp": group(step) // 2, "seq": lax.rem(group(step), 2) * 2 + turn}
    tokens, model = hidden.shape
    slots = info_ref.shape[0]
    piece, units = tokens // 2, w_up.shape[1]
    cols, out_cols = up_ref.shape[2], out_ref.shape[2]
    act_cols = units // dp_size
    pairs = [
        (w_out_hbm, w_out),
        (x_hbm, x_own),
        (w_up_hbm, w_up),
        (w_down_hbm, w_down),
        (w_proj_hbm, w_proj),
    ]
    loads = [pltpu.make_async_copy(*pair, load_sem.at[at]) for at, pair in enumerate(pairs)]
    barrier = pltpu.get_barrier_semaphore()
    signal(barrier, other_core)
    each(1, groups, lambda step: signal(barrier, peer(step)))

    def head_rows(member, block):
        which = 1 - row if block == 0 else row
        return pl.ds(pl.multiple_of((which * 2 + member) * out_cols, out_cols), out_cols)

    def row_lanes(member, half):
        return pl.ds(pl.multiple_of((member + 2 * half) * piece, piece), piece)

    def half_of(half):
        return pl.ds(pl.multiple_of(half * piece, piece), piece)

    def heads_here(block, half):
        return pltpu.make_async_copy(
            o_hbm.at[pl.ds(block * out_cols, out_cols), row_lanes(turn, half)],
            attended.at[head_rows(turn, block), half_of(half)],
            head_load.at[block, half],
        )

    def heads_there(block, half, sender):
        return remote(
            o_hbm.at[pl.ds(block * out_cols, out_cols), row_lanes(1 - sender, half)],
            attended.at[head_rows(sender, block), half_of(half)],
            head_send.at[block, half],
            head_recv.at[block, half],
            other_core,
        )

    quarters = [(block, half) for half in range(2) for block in range(2)]
    for block, half in quarters:
        heads_here(block, half).start()
    for load in loads:
        load.start()
    pl.semaphore_wait(barrier, groups)
    for block, half in quarters:
        heads_there(block, half, turn).start()

    def members(rows, parts):
        seg = seg_ref[rows, :]
        lane = lax.broadcasted_iota(jnp.int32, seg.shape, 1)
        hit = (lax.rem(lane, 16) == seg) & (lane < 16 * parts)
        return jnp.where(hit, 1.0, 0.0)

    gain = gain_ref[...].reshape(1, model)
    loads[0].wait()
    loads[1].wait()
    per_half = piece // TILE

    def attended_tile(at):
        @pl.when(lax.rem(at, per_half) == 0)
        def _():
            for block in range(2):
                heads_here(block, at // per_half).wait()
                heads_there(block, at // per_half, 1 - turn).wait_recv()

        rows = tile_part(at)
        left = jnp.transpose(attended[:, rows].astype(F32)).astype(BF16)
        value = x_own[rows, :].astype(F32) + dot(left, w_out[...])
        hidden[rows, :] = value
        scale = lax.rsqrt(jnp.mean(value * value, axis=1, keepdims=True) + EPS)
        value = value * scale * gain
        normed_two[rows, :] = value.astype(BF16)
        normed_t[:, rows] = jnp.transpose(value).astype(BF16)

    each(0, tokens // TILE, attended_tile)
    loads[2].wait()

    def up(at, slot):
        raw[slot] = dot(normed_two[...], w_up[:, tile_part(at)])

    def bend(at, slot):
        lanes = tile_part(at)
        value = raw[slot]
        below = 0.5 + 0.5 * lax.erf(value * (0.5**0.5))
        density = jnp.exp(-0.5 * value * value) * 0.3989422804014327
        act[:, lanes] = (value * below).astype(BF16)
        slope[:, lanes] = (below + value * density).astype(BF16)

    strips = units // TILE

    def two_strips(at):
        up(2 * at + 1, 1)
        bend(2 * at, 0)
        up(lax.rem(2 * at + 2, strips), 0)
        bend(2 * at + 1, 1)

    up(0, 0)
    each(0, strips // 2, two_strips)
    loads[3].wait()
    member = jnp.transpose(members(pl.ds(0, tokens), 1))[:16].astype(BF16)
    sum_parts[...] = jnp.zeros_like(sum_parts)

    def down(half):
        rows = pl.ds(pl.multiple_of(half * piece, piece), piece)
        value = hidden[rows, :] + dot(act[rows, :], w_down[...])
        total[rows, :] = value
        high = value.astype(BF16)
        rest = (value - high.astype(F32)).astype(BF16)
        left = members_t[:, rows]
        sum_parts[...] += dot(left, high) + dot(left, rest)

    members_t[...] = member
    each(0, 2, down)
    near_sums[turn] = sum_parts[:slots, :]

    def act_part(part):
        lanes = pl.ds(pl.multiple_of(part * act_cols, act_cols), act_cols)
        near_act[turn, part] = dot(members_t[...], act[:, lanes])[:slots]

    each(0, dp_size, act_part)

    def near(source):
        return [
            remote(
                buffer.at[source],
                buffer.at[source],
                near_send.at[kind],
                near_recv.at[kind],
                other_core,
            )
            for kind, buffer in enumerate((near_sums, near_act))
        ]

    for copy in near(turn):
        copy.start()
    mixed_ref[row] = total[pl.ds(pl.multiple_of(row * piece, piece), piece), :].astype(BF16)
    mixed_out[...] = total[pl.ds(pl.multiple_of((1 - row) * piece, piece), piece), :].astype(BF16)
    mixed_copy = lambda at: remote(
        mixed_out, mixed_ref.at[at], mixed_send.at[0], mixed_recv.at[0], other_chip
    )
    for copy in near(1 - turn):
        copy.wait_recv()
    info = info_ref[...]
    pooled = (near_sums[0] + near_sums[1]) / (info[:, 0:1] * 64.0 + info[:, 1:2])
    inbox[me] = jnp.concatenate(
        [
            jnp.concatenate([pooled[:, : model // 2], info], axis=1),
            jnp.concatenate([pooled[:, model // 2 :], jnp.zeros_like(info)], axis=1),
        ],
        axis=0,
    ).astype(BF16)

    def message(step, source):
        return remote(
            inbox.at[source], inbox.at[source], far_send.at[0, step], far_recv.at[0, source], peer(step)
        )

    def act_message(step, source):
        return remote(
            act_total.at[group(step) // 2],
            act_inbox.at[source],
            far_send.at[1, step],
            far_recv.at[1, source],
            peer(step),
        )

    each(1, groups, lambda step: message(step, me).start())
    act_total[...] = near_act[0] + near_act[1]
    act_inbox[me] = act_total[dp_at]
    loads[4].wait()
    each(1, groups, lambda step: message(step, group(step)).wait_recv())
    each(1, groups, lambda step: act_message(step, me).start())
    mixed_copy(row).start()
    loss_terms(inbox, w_proj, slots, loss_ref, pooled_ref, grad_proj_ref, grad_block_ref)

    def stacked(parts):
        parts = [part.astype(BF16) for part in parts]
        rest = jnp.zeros((128 - 16 * len(parts), parts[0].shape[1]), BF16)
        return jnp.concatenate(parts + [rest], axis=0)

    block = grad_block_ref[pl.ds(pl.multiple_of(me * slots, slots), slots), :]
    block = jnp.concatenate([block, jnp.zeros_like(block)], axis=0)
    block_b, block_parts = block.astype(BF16), stacked(three_parts(block))

    def grad_up(at):
        lanes = tile_part(at)
        grad_act = dot_nt(block_b, w_down[lanes, :])
        high = grad_act.astype(BF16).astype(F32)
        both = stacked([high, grad_act - high])
        for half in range(2):
            rows = half_of(half)
            spread = dot(members(rows, 2).astype(BF16), both)
            slope[rows, lanes] = (spread * slope[rows, lanes].astype(F32)).astype(BF16)

    each(0, units // TILE, grad_up)
    gain_sum[...] = jnp.zeros_like(gain_sum)

    def token_part(at):
        rows = pl.ds(pl.multiple_of(at * BLOCK, BLOCK), BLOCK)
        grad, value = total[rows, :], hidden[rows, :]
        scale = lax.rsqrt(jnp.mean(value * value, axis=1, keepdims=True) + EPS)
        scaled = gain * grad
        inner = jnp.mean(scaled * value, axis=1, keepdims=True)
        terms = grad * value * scale
        gain_sum[...] += jnp.sum(terms.reshape(BLOCK // 8, 8, model), axis=0)
        result = dot(members(rows, 3).astype(BF16), block_parts)
        result = result + scale * scaled - value * (scale * scale * scale * inner)
        total[rows, :] = result
        grad_b[rows, :] = result.astype(BF16)

    def att_copy(block, half, sender):
        return remote(
            grad_att.at[head_rows(1 - sender, block), half_of(half)],
            g_ref.at[pl.ds(block * out_cols, out_cols), row_lanes(sender, half)],
            att_send.at[block, half],
            att_recv.at[block, half],
            other_core,
        )

    def store(half):
        return pltpu.make_async_copy(
            total.at[half_of(half), :], grad_hbm.at[half_of(half), :], store_sem.at[half]
        )

    def token_half(half):
        rows = half_of(half)
        total[rows, :] = dot_nt(slope[rows, :], w_up[...])
        each(half * (piece // BLOCK), (half + 1) * (piece // BLOCK), token_part)
        store(half).start()
        grad_att[:, rows] = dot_nt(w_out[...], grad_b[rows, :]).astype(BF16)
        for block in range(2):
            att_copy(block, half, turn).start()

    each(0, 2, token_half)
    for block, half in quarters:
        mine = grad_att[head_rows(turn, block), half_of(half)]
        g_ref[pl.ds(block * out_cols, out_cols), row_lanes(turn, half)] = mine

    def up_box(kind, x):
        return act.at[pl.ds(0, model), pl.ds(pl.multiple_of((2 * kind + x) * cols, cols), cols)]

    def up_copy(x):
        return remote(up_box(0, x), up_box(1, x), core_send.at[0, x], core_recv.at[0, x], other_core)

    def out_copy(x):
        return remote(
            out_send.at[x], out_recv.at[x], core_send.at[1, x], core_recv.at[1, x], other_core
        )

    def out_part(x, core):
        starts = [(2 * x + side) * out_cols for side in range(2)]
        return jnp.where(core == 0, *(out_full[:, start : start + out_cols] for start in starts))

    strips = cols // TILE

    def up_strip(at):
        side, x = at // (2 * strips), lax.rem(at // strips, 2)
        strip = lax.rem(at, strips)
        core = jnp.where(side == 0, 1 - turn, turn)
        start = pl.multiple_of((2 * x + core) * cols + strip * TILE, TILE)
        value = dot(normed_t[...], slope[:, pl.ds(start, TILE)]).astype(BF16)

        @pl.when(side == 0)
        def _():
            act[:model, pl.ds(pl.multiple_of(x * cols + strip * TILE, TILE), TILE)] = value

            @pl.when(strip == strips - 1)
            def _():
                up_copy(x).start()

        @pl.when(side == 1)
        def _():
            up_ref[x, :, tile_part(strip)] = value

    each(0, 2 * strips, up_strip)
    out_full = dot(attended[...], grad_b[...])
    for x in range(2):
        out_send[x] = out_part(x, 1 - turn).astype(BF16)
        out_copy(x).start()
    each(2 * strips, 4 * strips, up_strip)
    for x in range(2):
        up_copy(x).wait_recv()
        out_copy(x).wait_recv()
        up_ref[x] = added(up_ref[x], act[:model, (2 + x) * cols : (3 + x) * cols])
        out_ref[x] = (out_part(x, turn) + out_recv[x].astype(F32)).astype(BF16)

    mixed_copy(1 - row).wait_recv()
    each(1, groups, lambda step: act_message(step, group(step)).wait_recv())
    act_all_ref[...] = act_inbox[...]
    for block, half in quarters:
        att_copy(block, half, 1 - turn).wait_recv()
        att_copy(block, half, turn).wait_send()
        heads_there(block, half, turn).wait_send()
    for x in range(2):
        up_copy(x).wait_send()
        out_copy(x).wait_send()
    for copy in near(turn):
        copy.wait_send()
    mixed_copy(row).wait_send()
    each(1, groups, lambda step: message(step, me).wait_send())
    each(1, groups, lambda step: act_message(step, me).wait_send())
    for half in range(2):
        store(half).wait()


def feed_forward_and_loss(info, seg_columns, gain, w_out, x_own, w_up, w_down, w_proj, o_t, dp_size):
    slots = info.shape[0]
    tokens, model = x_own.shape
    units, piece = w_up.shape[1], tokens // 2
    cols, out_cols = units // 4, model // 4
    groups, many, act_cols = 2 * dp_size, 2 * dp_size * slots, units // dp_size
    vmem, anywhere = pl.BlockSpec(memory_space=pltpu.VMEM), pl.BlockSpec(memory_space=pl.ANY)
    dma, shape = pltpu.SemaphoreType.DMA, jax.ShapeDtypeStruct
    return pl.pallas_call(
        functools.partial(middle_kernel, dp_size),
        in_specs=[vmem] * 3 + [anywhere] * 6,
        out_specs=[vmem] * 7 + [anywhere] + [vmem] * 3,
        out_shape=[
            shape((2, piece, model), BF16),
            shape((1, 1), F32),
            shape((many, model), BF16),
            shape((many, w_proj.shape[1]), BF16),
            shape((many, model), F32),
            shape((groups, slots, act_cols), F32),
            shape((2 * out_cols, 2 * tokens), BF16),
            shape((tokens, model), F32),
            shape((8, model), F32),
            shape((2, model, cols), BF16),
            shape((2, model, out_cols), BF16),
        ],
        scratch_shapes=[
            pltpu.VMEM((model, model), BF16),
            pltpu.VMEM((tokens, model), BF16),
            pltpu.VMEM((model, units), BF16),
            pltpu.VMEM((units, model), BF16),
            pltpu.VMEM(w_proj.shape, BF16),
            pltpu.VMEM((model, tokens), BF16),
            pltpu.VMEM((tokens, model), F32),
            pltpu.VMEM((tokens, model), BF16),
            pltpu.VMEM((model, tokens), BF16),
            pltpu.VMEM((tokens, units), BF16),
            pltpu.VMEM((tokens, units), BF16),
            pltpu.VMEM((tokens, model), F32),
            pltpu.VMEM((2, tokens, TILE), F32),
            pltpu.VMEM((16, tokens), BF16),
            pltpu.VMEM((16, model), F32),
            pltpu.VMEM((piece, model), BF16),
            pltpu.VMEM((2, slots, model), F32),
            pltpu.VMEM((2, dp_size, slots, act_cols), F32),
            pltpu.VMEM((dp_size, slots, act_cols), F32),
            pltpu.VMEM((groups, 2 * slots, model // 2 + 128), BF16),
            pltpu.VMEM((groups, slots, act_cols), F32),
            pltpu.VMEM((tokens, model), BF16),
            pltpu.VMEM((model, tokens), BF16),
            pltpu.VMEM((2, model, out_cols), BF16),
            pltpu.VMEM((2, model, out_cols), BF16),
            dma((5,)),
            dma((2,)),
            dma((2, 2)),
            dma((2, 2)),
            dma((2, 2)),
            dma((2,)),
            dma((2,)),
            dma((2, groups)),
            dma((2, groups)),
            dma((1,)),
            dma((1,)),
            dma((2, 2)),
            dma((2, 2)),
            dma((2, 2)),
            dma((2, 2)),
        ],
        compiler_params=pltpu.CompilerParams(
            collective_id=4, has_side_effects=True, vmem_limit_bytes=63 * MIB
        ),
        cost_estimate=pl.CostEstimate(
            flops=8 * units * tokens * model,
            bytes_accessed=24 * MIB,
            transcendentals=2 * tokens * units,
        ),
        name="feed_forward_and_loss",
    )(
        info,
        seg_columns,
        gain,
        w_out,
        x_own,
        w_up,
        w_down,
        w_proj,
        o_t,
    )


def tail_kernel(
    dp_size,
    bucket_count,
    gain_ref,
    ffn_ref,
    last_ref,
    late_ref,
    pooled_ref,
    proj_ref,
    block_ref,
    act_ref,
    diag_ref,
    w_hbm,
    d_hbm,
    x_hbm,
    hidden_hbm,
    own_ref,
    chip_in,
    total_ref,
    g_qkv_ref,
    g_proj_ref,
    g_down_ref,
    w_ref,
    d_ref,
    x_ref,
    hidden_ref,
    near_out,
    near_in,
    part,
    gain_sum,
    chip_out,
    last_far,
    turned,
    seq_box,
    dp_box,
    load_sem,
    near_send,
    near_recv,
    chip_send,
    chip_recv,
    last_send,
    last_recv,
    seq_send,
    seq_recv,
    dp_send,
    dp_recv,
):
    seq_size = 4
    dp_at, seq_at = lax.axis_index("dp"), lax.axis_index("seq")
    row, turn = seq_at // 2, lax.rem(seq_at, 2)
    along_seq = lambda step: {"dp": dp_at, "seq": lax.rem(seq_at + step, seq_size)}
    along_dp = lambda step: {"dp": lax.rem(dp_at + step, dp_size), "seq": seq_at}
    other_core = {"dp": dp_at, "seq": row * 2 + 1 - turn}
    other_chip = {"dp": dp_at, "seq": lax.rem(seq_at + 2, seq_size)}
    model, piece = w_ref.shape[0], own_ref.shape[0]
    rows = g_proj_ref.shape[0]
    parts = TILE // BLOCK
    barrier = pltpu.get_barrier_semaphore()
    each(1, seq_size, lambda step: signal(barrier, along_seq(step)))
    each(1, dp_size, lambda step: signal(barrier, along_dp(step)))
    loads = [
        pltpu.make_async_copy(source, target, load_sem.at[at])
        for at, (source, target) in enumerate(
            [(w_hbm, w_ref), (d_hbm, d_ref), (x_hbm, x_ref), (hidden_hbm, hidden_ref)]
        )
    ]
    for load in loads:
        load.start()

    def product(member, at):
        which = jnp.where(at < 2, 1 - row, row)
        start = pl.multiple_of((member + 2 * which) * piece + lax.rem(at, 2) * TILE, TILE)
        return dot(w_ref[...], d_ref[:, pl.ds(start, TILE)])

    def near_copy(at):
        return remote(near_out.at[at], near_in.at[at], near_send.at[at], near_recv.at[at], other_core)

    def chip_copy(at):
        return remote(chip_out.at[at], chip_in.at[at], chip_send.at[at], chip_recv.at[at], other_chip)

    def last_copy(step, source):
        to = pl.ds(pl.multiple_of(lax.rem(dp_at + step, dp_size) * rows, rows), rows)
        return remote(
            last_ref.at[to, :], last_far.at[source], last_send.at[step], last_recv.at[source], along_dp(step)
        )

    gain_sum[...] = jnp.zeros_like(gain_sum)
    gain = gain_ref[...].reshape(1, model)
    loads[0].wait()
    loads[1].wait()
    def send_near(at):
        near_out[at] = product(1 - turn, at).astype(BF16)

        @pl.when(at == 0)
        def _():
            pl.semaphore_wait(barrier, seq_size - 1 + dp_size - 1)

        near_copy(at).start()

    def quarter(at):
        part[...] = product(turn, at)

        @pl.when(at == 0)
        def _():
            each(1, dp_size, lambda step: last_copy(step, dp_at).start())
            loads[2].wait()
            loads[3].wait()

        @pl.when(at < 3)
        def _():
            send_near(at + 1)

        near_copy(at).wait_recv()
        which = jnp.where(at < 2, 1 - row, row)

        def block(sub):
            lanes = pl.ds(pl.multiple_of(sub * BLOCK, BLOCK), BLOCK)
            place = pl.multiple_of(lax.rem(at, 2) * TILE + sub * BLOCK, BLOCK)
            there = pl.ds(pl.multiple_of(which * piece + place, BLOCK), BLOCK)
            grad = jnp.transpose(part[:, lanes] + near_in[at, :, lanes].astype(F32))
            x = x_ref[there, :].astype(F32)
            scale = lax.rsqrt(jnp.mean(x * x, axis=1, keepdims=True) + EPS)
            scaled = gain * grad
            inner = jnp.mean(scaled * x, axis=1, keepdims=True)
            gain_sum[...] += jnp.sum((grad * x * scale).reshape(BLOCK // 8, 8, model), axis=0)
            result = hidden_ref[there, :] + scale * scaled - x * (scale * scale * scale * inner)

            @pl.when(at < 2)
            def _():
                chip_out[at * parts + sub] = result.astype(BF16)
                chip_copy(at * parts + sub).start()

            @pl.when(at >= 2)
            def _():
                own_ref[pl.ds(place, BLOCK), :] = result

        each(0, parts, block)

    each(0, 1, send_near)
    each(0, 4, quarter)

    heads = diag_ref.shape[0]
    sums = diag_ref[...].reshape(heads * 8, 2 * BLOCK)
    sums = [value.astype(BF16) for value in three_parts(sums)]
    row_at = lax.rem(lax.broadcasted_iota(jnp.int32, (heads * 8, 128), 0), 8)
    lane = lax.broadcasted_iota(jnp.int32, (2 * BLOCK, 128), 1)
    place = lax.broadcasted_iota(jnp.int32, (2 * BLOCK, 128), 0)
    place = jnp.where(place < BLOCK, place, place - 2 * BLOCK)
    table = jnp.zeros((heads * 8, 128), F32)
    for band in range(BANDS):
        offset = (band - BANDS // 2) * BLOCK - place
        onehot = jnp.where(bucket_of(offset, bucket_count // 2) == lane, 1.0, 0.0).astype(BF16)
        found = dot(sums[0], onehot) + dot(sums[1], onehot) + dot(sums[2], onehot)
        table = table + jnp.where(row_at == band, found, 0.0)
    table = jnp.sum(table.reshape(heads, 8, 128), axis=1)
    run = heads // 2
    table = jnp.concatenate(
        [
            jnp.where(
                (1 - row) * 2 + turn == group,
                table[:run],
                jnp.where(row * 2 + turn == group, table[run:], 0.0),
            )
            for group in range(4)
        ],
        axis=0,
    )

    def as_rows(value):
        value = jnp.sum(value, axis=0, keepdims=True)
        return [value[:, at : at + 128] for at in range(0, model, 128)]

    value = jnp.concatenate(as_rows(gain_sum[...]) + as_rows(ffn_ref[...]) + [table], axis=0)

    def stage_total(value, at, size, where, box, send, receive):
        box[at] = value
        copy = lambda step, source: remote(
            box.at[source], box.at[source], send.at[step], receive.at[source], where(step)
        )
        each(1, size, lambda step: copy(step, at).start())
        each(1, size, lambda step: copy(step, lax.rem(at + step, size)).wait_recv())
        total = box[0]
        for source in range(1, size):
            total = total + box[source]
        each(1, size, lambda step: copy(step, at).wait_send())
        return total

    value = stage_total(value, seq_at, seq_size, along_seq, seq_box, seq_send, seq_recv)
    total_ref[...] = stage_total(value, dp_at, dp_size, along_dp, dp_box, dp_send, dp_recv)

    own_rows = pl.ds(pl.multiple_of(dp_at * rows, rows), rows)
    out_cols = g_proj_ref.shape[1]
    own_cols = pl.ds(pl.multiple_of(seq_at * out_cols, out_cols), out_cols)
    turned[0] = jnp.transpose(pooled_ref[...].astype(F32))
    turned[1] = jnp.transpose(proj_ref[...].astype(F32))
    turned[2] = jnp.transpose(block_ref[...])
    g_proj_ref[...] = dot_nt(turned[0, own_rows, :].astype(BF16), turned[1, own_cols, :].astype(BF16))
    act = jnp.transpose(act_ref[...].reshape(pooled_ref.shape[0], act_ref.shape[2]))
    block = turned[2, own_cols, :].astype(BF16)
    high = act.astype(BF16)
    rest = (act - high.astype(F32)).astype(BF16)
    g_down_ref[...] = dot_nt(block, high) + dot_nt(block, rest)

    each(1, dp_size, lambda step: last_copy(step, lax.rem(dp_at + step, dp_size)).wait_recv())
    last_far[dp_at] = jnp.zeros(last_far.shape[1:], BF16)
    last = last_ref[own_rows, :].astype(F32)
    for source in range(dp_size):
        last = last + last_far[source].astype(F32)
    late = [late_ref[which] for which in range(late_ref.shape[0])] + [last]
    width = late_ref.shape[2] // 3
    for kind in range(3):
        g_qkv_ref[kind] = jnp.concatenate(
            [value[:, kind * width : (kind + 1) * width] for value in late], axis=1
        )
    for at in range(2 * parts):
        chip_copy(at).wait_recv()
    for at in range(4):
        near_copy(at).wait_send()
    for at in range(2 * parts):
        chip_copy(at).wait_send()
    each(1, dp_size, lambda step: last_copy(step, dp_at).wait_send())


def token_gradients(
    d_qkv, w_qkv, x_own, grad_hidden, gain, gain_ffn, last, late, pooled, proj, block, act, diag, buckets, dp_size
):
    tokens, model = x_own.shape
    piece, many = tokens // 2, pooled.shape[0]
    rows, out_cols = model // dp_size, model // 4
    run, width = late.shape[0] + 1, late.shape[2] // 3
    vmem, anywhere = pl.BlockSpec(memory_space=pltpu.VMEM), pl.BlockSpec(memory_space=pl.ANY)
    dma, shape = pltpu.SemaphoreType.DMA, jax.ShapeDtypeStruct
    return pl.pallas_call(
        functools.partial(tail_kernel, dp_size, buckets),
        in_specs=[vmem] * 9 + [anywhere] * 4,
        out_specs=[vmem] * 6,
        out_shape=[
            shape((piece, model), F32),
            shape((piece // BLOCK, BLOCK, model), BF16),
            shape((24, 128), F32),
            shape((3, rows, run * width), F32),
            shape((rows, out_cols), F32),
            shape((out_cols, act.shape[2]), F32),
        ],
        scratch_shapes=[
            pltpu.VMEM(w_qkv.shape, BF16),
            pltpu.VMEM(d_qkv.shape, BF16),
            pltpu.VMEM(x_own.shape, BF16),
            pltpu.VMEM(grad_hidden.shape, F32),
            pltpu.VMEM((4, model, TILE), BF16),
            pltpu.VMEM((4, model, TILE), BF16),
            pltpu.VMEM((model, TILE), F32),
            pltpu.VMEM((8, model), F32),
            pltpu.VMEM((piece // BLOCK, BLOCK, model), BF16),
            pltpu.VMEM((dp_size, rows, last.shape[1]), BF16),
            pltpu.VMEM((3, model, many), F32),
            pltpu.VMEM((4, 24, 128), F32),
            pltpu.VMEM((dp_size, 24, 128), F32),
            dma((4,)),
            dma((4,)),
            dma((4,)),
            dma((piece // BLOCK,)),
            dma((piece // BLOCK,)),
            dma((dp_size,)),
            dma((dp_size,)),
            dma((4,)),
            dma((4,)),
            dma((dp_size,)),
            dma((dp_size,)),
        ],
        compiler_params=pltpu.CompilerParams(
            collective_id=3, has_side_effects=True, vmem_limit_bytes=63 * MIB
        ),
        cost_estimate=pl.CostEstimate(
            flops=2 * d_qkv.shape[0] * d_qkv.shape[1] * model,
            bytes_accessed=16 * MIB,
            transcendentals=0,
        ),
        name="token_gradients",
    )(
        gain,
        gain_ffn,
        last,
        late,
        pooled,
        proj,
        block,
        act,
        diag,
        w_qkv,
        d_qkv,
        x_own,
        grad_hidden,
    )


def finish_kernel(own_ref, other_ref, small_ref, *refs):
    sources, (tokens_ref, attn_ref, ffn_ref, table_ref), targets = refs[:6], refs[6:10], refs[10:]
    lanes = attn_ref.shape[0] // 128
    for first, target in ((0, attn_ref), (lanes, ffn_ref)):
        parts = [small_ref[first + at : first + at + 1, :] for at in range(lanes)]
        target[...] = jnp.concatenate(parts, axis=1).reshape(target.shape)
    table_ref[...] = small_ref[2 * lanes : 2 * lanes + table_ref.shape[0], : table_ref.shape[1]]
    row = lax.axis_index("seq") // 2
    tokens_ref[row] = own_ref[...]

    def widen(at):
        rows = pl.ds(pl.multiple_of(at * BLOCK, BLOCK), BLOCK)
        tokens_ref[1 - row, rows, :] = other_ref[at].astype(F32)

    each(0, other_ref.shape[0], widen)
    for kind in range(3):
        targets[kind][...] = sources[0][kind]
    for source, target in zip(sources[1:], targets[3:]):
        target[...] = source[...]


def finish(own, other, small, table_shape, g_qkv, *rest):
    piece, model = own.shape
    vmem = pl.BlockSpec(memory_space=pltpu.VMEM)
    shape = lambda like: jax.ShapeDtypeStruct(like.shape, like.dtype)
    return pl.pallas_call(
        finish_kernel,
        in_specs=[vmem] * (4 + len(rest)),
        out_specs=[vmem] * (7 + len(rest)),
        out_shape=[jax.ShapeDtypeStruct((2, piece, model), F32)]
        + [jax.ShapeDtypeStruct((model,), F32)] * 2
        + [jax.ShapeDtypeStruct(table_shape, F32)]
        + [jax.ShapeDtypeStruct(g_qkv.shape[1:], F32)] * 3
        + [shape(value) for value in rest],
        compiler_params=pltpu.CompilerParams(vmem_limit_bytes=60 * MIB),
        name="finish",
    )(own, other, small, g_qkv, *rest)


def normed(inputs, gain_vec):
    return inputs * lax.rsqrt(jnp.mean(inputs * inputs, axis=-1, keepdims=True) + EPS) * gain_vec


def norm_back(inputs, gain_vec, grads_in):
    scale = lax.rsqrt(jnp.mean(inputs * inputs, axis=-1, keepdims=True) + EPS)
    gain_grad = jnp.sum(grads_in * inputs * scale, axis=0)
    scaled = gain_vec * grads_in
    inner = jnp.mean(scaled * inputs, axis=-1, keepdims=True)
    return scale * scaled - inputs * (scale * scale * scale * inner), gain_grad


def on_device(
    tokens,
    segment_ids,
    pair_ids,
    w_query,
    w_key,
    w_value,
    w_out,
    w_up,
    w_down,
    w_proj,
    gain_attn,
    gain_ffn,
    rel_bias,
):
    _, piece, model_width = tokens.shape
    bucket_count, head_count = rel_bias.shape
    slots = pair_ids.shape[1]
    dp_size, seq_size = lax.axis_size("dp"), lax.axis_size("seq")
    half = seq_size // 2
    length = piece * seq_size
    heads = head_count // half
    width = model_width // head_count
    dp_at, seq_at = lax.axis_index("dp"), lax.axis_index("seq")
    row, turn = seq_at // half, lax.rem(seq_at, half)
    across = [(i, (i + half) % seq_size) for i in range(seq_size)]

    def by_row(own, other):
        return jnp.where(row == 0, own, other), jnp.where(row == 0, other, own)

    def among(step):
        return [(i, i // half * half + (i % half + step) % half) for i in range(seq_size)]

    def trade(own, send_to):
        entries = [own] * half
        for step in range(1, half):
            got = lax.ppermute(send_to(lax.rem(turn + step, half)), "seq", among(step))
            source = lax.rem(turn + half - step, half)
            entries = [jnp.where(source == j, got, entry) for j, entry in enumerate(entries)]
        return entries

    def pick(value, at, size, dim):
        return lax.dynamic_slice_in_dim(value, at * size, size, dim)

    def pieces_of(value, member, dim):
        return jnp.concatenate(
            [pick(value, member, piece, dim), pick(value, member + half, piece, dim)], axis=dim
        )

    def in_row_order(entries, dim):
        halves = [jnp.split(entry, 2, axis=dim) for entry in entries]
        return jnp.concatenate([pair[0] for pair in halves] + [pair[1] for pair in halves], axis=dim)

    def own_pieces(local):
        own = lax.dynamic_index_in_dim(local, row, 0, keepdims=False)
        other = lax.dynamic_index_in_dim(local, 1 - row, 0, keepdims=False)
        return jnp.concatenate(by_row(own, lax.ppermute(other, "seq", across)), axis=0)

    def whole_row(pair):
        return in_row_order(trade(pair, lambda member: pair), 0)

    def hand_back(pair, kind):
        own, other = pick(pair, row, piece, 0), pick(pair, 1 - row, piece, 0)
        return jnp.stack(by_row(own, lax.ppermute(other.astype(kind), "seq", across).astype(own.dtype)))

    aligned = seq_size == 4 and heads % 2 == 0
    blocks = 2 if aligned else 1
    block_heads = heads // blocks
    columns, block_columns = heads * width, block_heads * width

    def block_at(block):
        return (1 - row if block == 0 else row) if aligned else 0

    def cut(value, member, size, dim):
        parts = [pick(value, block_at(block) * half + member, size, dim) for block in range(blocks)]
        return jnp.concatenate(parts, axis=dim)

    if aligned:
        qkv_t, normed_t, x_pair, seg_row, w_own, info, seg_columns = gather_and_project(
            tokens, segment_ids, pair_ids, gain_attn, w_query, w_key, w_value, heads
        )
    else:
        x_pair, seg_own = own_pieces(tokens), own_pieces(segment_ids)
        x_row, seg_row = whole_row(x_pair), whole_row(seg_own)[None]
        w_qkv = [cut(weight, turn, block_columns, 1) for weight in (w_query, w_key, w_value)]
        w_qkv = [weight.reshape(model_width, heads, width) for weight in w_qkv]
        w_qkv = jnp.stack(w_qkv, axis=2).reshape(model_width, 3 * columns)
        normed_one = normed(x_row.astype(F32), gain_attn).astype(BF16)
        qkv_t = jnp.einsum("dc,td->ct", w_qkv, normed_one, preferred_element_type=F32).astype(BF16)
        x_own = x_pair.astype(F32)
        slot_ids = jnp.arange(slots, dtype=jnp.int32)
        counts = jnp.sum((seg_row == slot_ids[:, None]).astype(jnp.int32), axis=1)
        own_pairs = lax.dynamic_index_in_dim(pair_ids, row, 0, keepdims=False)
        info = jnp.stack([counts // 64, counts % 64, own_pairs], axis=1).astype(F32)
        info = jnp.concatenate([info, jnp.zeros((slots, 125), F32)], axis=1)
    qkv_t = qkv_t.reshape(heads, 3, width, length)
    table = cut(rel_bias, turn, block_heads, 1)
    onehot = (
        bucket_of(diagonal_offsets(), bucket_count // 2)[:, :, None]
        == jnp.arange(bucket_count, dtype=jnp.int32)
    ).astype(F32)
    diag = jnp.einsum("txb,bh->htx", onehot, table, precision=lax.Precision.HIGHEST)
    diag = jnp.concatenate([diag, jnp.zeros((heads, 8 - BANDS, 2 * BLOCK), F32)], axis=1)
    o_t, o_b, inverse, probs = attention_forward(slots, qkv_t, seg_row, diag)

    def heads_to_tokens(value):
        entries = trade(pieces_of(value, turn, 1), lambda member: pieces_of(value, member, 1))
        parts = [jnp.split(entry, blocks, axis=0) for entry in entries]
        if aligned:
            parts = [by_row(part[1], part[0]) for part in parts]
        return jnp.concatenate([part[block] for block in range(blocks) for part in parts], axis=0)

    def tokens_to_heads(value):
        own = cut(value, turn, block_columns, 0)
        return in_row_order(trade(own, lambda member: cut(value, member, block_columns, 0)), 1)

    if aligned:
        (
            mixed,
            loss,
            pooled,
            grad_proj,
            grad_block_all,
            every_act,
            g_t,
            grad_hidden,
            grad_gain_ffn,
            up_sum,
            out_sum,
        ) = feed_forward_and_loss(
            info,
            seg_columns,
            gain_ffn,
            w_out,
            x_pair,
            w_up,
            w_down,
            w_proj,
            o_b.reshape(columns, length),
            dp_size,
        )
        d_qkv, diag_grads, g_up, g_out, late, last = attention_backward_and_sums(
            qkv_t,
            g_t.reshape(heads, width, length),
            o_t,
            inverse,
            probs,
            normed_t,
            up_sum,
            out_sum,
            dp_size,
        )
        own, other, small, g_qkv, g_proj, g_down = token_gradients(
            d_qkv.reshape(-1, length),
            w_own,
            x_pair,
            grad_hidden,
            gain_attn,
            grad_gain_ffn,
            last,
            late,
            pooled,
            grad_proj,
            grad_block_all,
            every_act,
            diag_grads,
            bucket_count,
            dp_size,
        )
        (
            grad_tokens,
            grad_gain_attn,
            grad_gain_ffn,
            table_grad,
            g_query,
            g_key,
            g_value,
            mixed,
            g_up,
            g_out,
            g_proj,
            g_down,
        ) = finish(
            own, other, small, (head_count, bucket_count), g_qkv, mixed, g_up, g_out, g_proj, g_down
        )
        g_down, table_grad = g_down.T, table_grad.T
    else:
        attended_t = heads_to_tokens(o_b.reshape(columns, length))
        hidden = x_own + jnp.einsum("ct,cd->td", attended_t, w_out, preferred_element_type=F32)
        normed_two = normed(hidden, gain_ffn).astype(BF16)
        up_proj = dot(normed_two, w_up)
        below = 0.5 * (1.0 + lax.erf(up_proj * (0.5**0.5)))
        act = (up_proj * below).astype(BF16)
        slope = (below + up_proj * jnp.exp(-0.5 * up_proj * up_proj) * 0.3989422804014327).astype(BF16)
        block_out = hidden + dot(act, w_down)
        mixed = hand_back(block_out.astype(BF16), BF16)
        member = (seg_own[None, :] == slot_ids[:, None]).astype(F32)
        sums = jnp.dot(member, block_out, precision=lax.Precision.HIGHEST)
        act_sums = dot(member.astype(BF16), act)

        loss, pooled, grad_proj, grad_block_all, every_act = loss_head(
            sums, act_sums, info, w_proj, dp_size, seq_size
        )
        grad_seg = lax.dynamic_slice_in_dim(grad_block_all, (dp_at * 2 + row) * slots, slots, 0)

        grad_act = dot_nt(grad_seg.astype(BF16), w_down)
        act_high = grad_act.astype(BF16)
        act_low = (grad_act - act_high.astype(F32)).astype(BF16)
        member_t = member.T.astype(BF16)
        spread = dot(
            jnp.concatenate([member_t, member_t], axis=1),
            jnp.concatenate([act_high, act_low], axis=0),
        )
        grad_up = (spread * slope.astype(F32)).astype(BF16)
        grad_wup = lax.dot_general(
            normed_two, grad_up, (((0,), (0,)), ((), ())), preferred_element_type=F32
        ).astype(BF16)
        grad_hidden, grad_gain_ffn = norm_back(hidden, gain_ffn, dot_nt(grad_up, w_up))
        grad_hidden = grad_hidden + jnp.dot(member.T, grad_seg, precision=lax.Precision.HIGHEST)
        grad_hidden_b = grad_hidden.astype(BF16)
        grad_wout = dot(attended_t, grad_hidden_b).astype(BF16)
        grad_att_t = dot_nt(w_out, grad_hidden_b).astype(BF16)
        g_t = tokens_to_heads(grad_att_t).reshape(heads, width, length)
        d_qkv, diag_grads = attention_backward(qkv_t, g_t, o_t, inverse, probs)
        every_act = every_act.reshape(-1, every_act.shape[2])
        proj_rows, proj_cols = model_width // dp_size, w_proj.shape[1] // seq_size
        g_proj = lax.dot_general(
            lax.dynamic_slice_in_dim(pooled, dp_at * proj_rows, proj_rows, 1),
            lax.dynamic_slice_in_dim(grad_proj, seq_at * proj_cols, proj_cols, 1),
            (((0,), (0,)), ((), ())),
            preferred_element_type=F32,
        )
        down_rows, down_cols = w_down.shape[0] // dp_size, model_width // seq_size
        g_down = lax.dot_general(
            every_act,
            lax.dynamic_slice_in_dim(grad_block_all, seq_at * down_cols, down_cols, 1)
            .astype(BF16)
            .astype(F32),
            (((0,), (0,)), ((), ())),
            precision=lax.Precision.HIGHEST,
        )
        table_part = jnp.einsum(
            "htx,txb->bh", diag_grads[:, :BANDS], onehot, precision=lax.Precision.HIGHEST
        )
        table_grad = jnp.zeros((bucket_count, head_count), F32)
        for block in range(blocks):
            table_grad = lax.dynamic_update_slice_in_dim(
                table_grad,
                table_part[:, block * block_heads : (block + 1) * block_heads],
                turn * block_heads,
                1,
            )
        def packed(gain_attn_part):
            small = jnp.concatenate([gain_attn_part, grad_gain_ffn, table_grad.reshape(-1)])
            return jnp.concatenate([small, jnp.zeros((-small.shape[0] % 1024,), F32)]).reshape(-1, 128)

        d_qkv = d_qkv.reshape(3 * columns, length)

        def owner_sum(value):
            value = lax.psum_scatter(value, "dp", scatter_dimension=0, tiled=True)
            return lax.psum_scatter(value, "seq", scatter_dimension=1, tiled=True).astype(F32)

        def own_columns(value):
            full = jnp.zeros((model_width, model_width), BF16)
            return lax.dynamic_update_slice_in_dim(full, value, turn * columns, 1)

        grad_w = lax.dot_general(
            normed_one, d_qkv, (((0,), (1,)), ((), ())), preferred_element_type=F32
        ).astype(BF16)
        grad_w = grad_w.reshape(model_width, heads, 3, width)
        g_query, g_key, g_value = [
            owner_sum(own_columns(grad_w[:, :, part].reshape(model_width, columns)))
            for part in range(3)
        ]
        g_up, g_out = owner_sum(grad_wup), owner_sum(grad_wout)
        grad_normed_part = jnp.einsum("ct,dc->td", d_qkv, w_qkv, preferred_element_type=F32)
        grad_normed = pieces_of(grad_normed_part, turn, 0)
        for step in range(1, half):
            send = pieces_of(grad_normed_part, lax.rem(turn + step, half), 0).astype(BF16)
            grad_normed = grad_normed + lax.ppermute(send, "seq", among(step)).astype(F32)
        grad_x, grad_gain_attn = norm_back(x_own, gain_attn, grad_normed)
        grad_tokens = hand_back(grad_hidden + grad_x, BF16)
        small = total_over_all(packed(grad_gain_attn), dp_size, seq_size)
        small = small.reshape(-1)
        grad_gain_attn, grad_gain_ffn = small[:model_width], small[model_width : 2 * model_width]
        table_grad = small[2 * model_width :][: bucket_count * head_count]
        table_grad = table_grad.reshape(bucket_count, head_count)
    return (
        mixed,
        loss[0, 0],
        grad_tokens,
        g_query,
        g_key,
        g_value,
        g_out,
        g_up,
        g_down,
        g_proj,
        grad_gain_attn,
        grad_gain_ffn,
        table_grad,
    )


def solution(mesh):
    in_specs = (P("dp", "seq", None), P("dp", "seq"), P("dp", None)) + (P(),) * 10
    out_specs = (
        (P("dp", "seq", None), P(), P("dp", "seq", None)) + (P("dp", "seq"),) * 7 + (P(),) * 3
    )
    return jax.shard_map(
        on_device, mesh=mesh, in_specs=in_specs, out_specs=out_specs, check_vma=False
    )
```
